32 devices in a mesh: groups: 2 (over x), expert: 8 (over z, y), replica: 2 (over core).
Axes of the slice: x: 2, y: 2, z: 4, core: 2. Of those that a mesh axis runs over, the one named last changes fastest.
Arguments:
- tiles: bfloat16 [1024, 12, 12, 128], P(('groups', 'expert', 'replica')), parts along dimension 0, may hold values from -6 to 6
- route: int32 [1024], P(('groups', 'expert', 'replica')), parts along dimension 0, may hold values from 0 to 7, as said below
- gate: float32 [1024], P(('groups', 'expert', 'replica')), parts along dimension 0, may hold values from 0.25 to 1
- conv_first: bfloat16 [8, 3, 3, 128, 128], P('expert'), may hold values from -0.1875 to 0.1875
- conv_second: bfloat16 [8, 3, 3, 128, 128], P('expert'), may hold values from -0.1875 to 0.1875
- cotangent: bfloat16 [1024, 8, 8, 128], P(('groups', 'expert', 'replica')), parts along dimension 0, may hold values from -6 to 6
Outputs:
- output: bfloat16 [1024, 8, 8, 128], P(('groups', 'expert', 'replica')), parts along dimension 0
- tiles_grad: bfloat16 [1024, 12, 12, 128], P(('groups', 'expert', 'replica')), parts along dimension 0
- first_grad: float32 [16, 3, 3, 128, 128], P(('groups', 'expert')), parts along dimension 0
- second_grad: float32 [16, 3, 3, 128, 128], P(('groups', 'expert')), parts along dimension 0
- gate_grad: float32 [1024], P(('groups', 'expert', 'replica')), parts along dimension 0
The draws below stay inside these ranges and needn't reach their ends.
There are 2 independent parts, one for each index of `groups`. The reference program is written for one: setup_inputs(seed, part) draws one part's arguments, and reference() takes and returns one part's arrays. A program takes and returns all parts, laid end to end along the dimension named above; an argument that names none is the same for every part. Nothing has to cross between parts.
Inputs may be any that keep to these rules, and one draw needn't show every extreme that they name: `route`: the 32 patches of one device name each expert at most 4 times, and one expert is named exactly 4 times by every device's patches.
All inputs are finite; a program needn't handle non-finite values.
Results may differ from the reference program's by a relative error of at most 0.0057.
Values may be sent and summed in bfloat16 or wider, within the bound.
No kernel may reach another device: no remote copies, remote signals or barrier semaphores. Data moves between devices by JAX's collectives and lax.ppermute only.
A program may use at most 64 MiB of HBM per device.

```python
import jax
import jax.numpy as jnp
from jax import lax

C = 128
PS = 8
P_DEV = 32
EXPERTS = 8
CAP = 4
TOKENS = 512
N_EXPERT = 8
N_REPLICA = 2


def draw_route(key, part):
    key = jax.random.fold_in(key, 11)
    key_bias, key_noise, key_full, key_order = jax.random.split(key, 4)
    source_count = N_EXPERT * N_REPLICA
    slot_count = N_EXPERT * CAP
    expert_bias = jax.random.permutation(key_bias, N_EXPERT).astype(jnp.int32) * 2
    full_expert = jax.random.randint(key_full, (), 0, N_EXPERT)
    noise_term = jax.random.randint(key_noise, (source_count, N_EXPERT, CAP), 0, 64)
    boost_term = jnp.where(jnp.arange(N_EXPERT) == full_expert, 4096, 0).astype(jnp.int32)
    scores_all = (noise_term + expert_bias[None, :, None] + boost_term[None, :, None]) * slot_count
    scores_all = scores_all + jnp.arange(slot_count, dtype=jnp.int32).reshape(1, N_EXPERT, CAP)
    chosen = lax.top_k(scores_all.reshape(source_count, slot_count), P_DEV)[1]
    expert_ids = (chosen // CAP).astype(jnp.int32)
    order_keys = jax.random.randint(key_order, (source_count, P_DEV), 0, 4096) * P_DEV + jnp.arange(P_DEV, dtype=jnp.int32)[None, :]
    order_index = jnp.argsort(order_keys, axis=1)
    shuffled = jnp.take_along_axis(expert_ids, order_index, axis=1)
    return shuffled.reshape(-1).astype(jnp.int32)


def shard_levels(stream_key, extent, cuts, low, top_value):
    def one(dim, blocks):
        draws = jax.random.uniform(jax.random.fold_in(jax.random.fold_in(stream_key, 6), dim), (blocks,), jnp.float32, low / len(cuts), top_value / len(cuts))
        return jnp.repeat(jnp.exp(draws), extent[dim] // blocks).reshape((-1,) + (1,) * (len(extent) - dim - 1))

    factor_of = one(*cuts[0])
    for cut in cuts[1:]:
        factor_of = factor_of * one(*cut)
    return factor_of


def scatter_about(own_key, dims, scale, bound, cuts=(), held_as=jnp.bfloat16):
    entries = scale * jax.random.normal(own_key, dims, jnp.float32)
    if cuts:
        entries = entries * shard_levels(own_key, dims, cuts, -0.22, 0.18)
    return jnp.clip(entries, -bound, bound).astype(held_as)


def setup_inputs(seed: int = 0, part: int = 0) -> dict:
    splits = jax.random.split(jax.random.key(seed), 7)
    own_keys = jax.random.split(jax.random.fold_in(splits[6], part), 7)
    tiles = scatter_about(own_keys[0], (TOKENS, PS + 4, PS + 4, C), 1.0, 6.0, ((0, 16),))
    route = draw_route(jax.random.fold_in(jax.random.fold_in(splits[6], part), 71), part)
    gate = jnp.clip(0.25 + 0.75 * jax.random.uniform(own_keys[2], (TOKENS,), jnp.float32) ** shard_levels(own_keys[2], (TOKENS,), ((0, 16),), -0.2, 0.2), 0.25, 1.0)
    conv_first = scatter_about(splits[3], (EXPERTS, 3, 3, C, C), (9 * C) ** -0.5, 0.1875, ((0, 8),))
    conv_second = scatter_about(splits[4], (EXPERTS, 3, 3, C, C), (9 * C) ** -0.5, 0.1875, ((0, 8),))
    cotangent = scatter_about(own_keys[5], (TOKENS, PS, PS, C), 1.0, 6.0, ((0, 16),))
    return {"tiles": tiles, "route": route, "gate": gate, "conv_first": conv_first, "conv_second": conv_second, "cotangent": cotangent}


LAYOUT = ('NHWC', 'HWIO', 'NHWC')
HIGHEST = lax.Precision.HIGHEST

def convolve(inputs, kernel):
    return lax.conv_general_dilated(inputs.astype(jnp.float32), kernel.astype(jnp.float32), (1, 1), 'VALID', dimension_numbers=LAYOUT, precision=HIGHEST)

def transpose_conv(gradient, kernel):
    padded = jnp.pad(gradient.astype(jnp.float32), ((0, 0), (2, 2), (2, 2), (0, 0)))
    flipped = jnp.transpose(kernel[::-1, ::-1], (0, 1, 3, 2))
    return convolve(padded, flipped)

def kernel_grad(inputs, gradient):
    height_out = gradient.shape[1]
    width_out = gradient.shape[2]
    pieces = []
    for row_shift in range(3):
        for col_shift in range(3):
            window = inputs[:, row_shift:row_shift + height_out, col_shift:col_shift + width_out, :].astype(jnp.float32)
            pieces.append(jnp.einsum('nijc,nijd->cd', window, gradient.astype(jnp.float32), precision=HIGHEST))
    stacked = jnp.stack(pieces)
    return stacked.reshape((3, 3) + stacked.shape[1:])

def silu_slope(pre_act):
    sigma_val = jax.nn.sigmoid(pre_act)
    return sigma_val * (1.0 + pre_act * (1.0 - sigma_val))

def reference(tiles, route, gate, conv_first, conv_second, cotangent):
    source_count = N_EXPERT * N_REPLICA
    per_source = route.reshape(source_count, P_DEV)
    onehot = (per_source[:, :, None] == jnp.arange(N_EXPERT, dtype=jnp.int32)[None, None, :]).astype(jnp.int32)
    rank_within = jnp.cumsum(onehot, axis=1) - 1
    slot_index = lax.optimization_barrier(jnp.sum(onehot * rank_within, axis=2))
    source_index = jnp.arange(source_count, dtype=jnp.int32)[:, None]
    flat_index = (per_source * (source_count * CAP) + source_index * CAP + slot_index).reshape(-1).astype(jnp.int32)
    total_slots = N_EXPERT * source_count * CAP
    scaled = (gate[:, None, None, None] * cotangent.astype(jnp.float32)).astype(jnp.bfloat16)

    def to_slots(values):
        blank_slots = jnp.zeros((total_slots,) + values.shape[1:], values.dtype)
        filled = blank_slots.at[flat_index].set(values)
        return filled.reshape((N_EXPERT, source_count * CAP) + values.shape[1:])

    def expert_work(operands):
        received, grads_in, kernel_one, kernel_two = operands
        pre_act = convolve(received, kernel_one)
        hidden = jax.nn.silu(pre_act).astype(jnp.bfloat16)
        result = convolve(hidden, kernel_two).astype(jnp.bfloat16)
        grad_hidden = transpose_conv(grads_in, kernel_two)
        grad_mid = (grad_hidden * silu_slope(pre_act)).astype(jnp.bfloat16)
        tile_grad = transpose_conv(grad_mid, kernel_one).astype(jnp.bfloat16)
        return (result, tile_grad, kernel_grad(received, grad_mid), kernel_grad(hidden, grads_in))
    results, tile_grads, first_grad, second_grad = lax.map(expert_work, (to_slots(tiles), to_slots(scaled), conv_first, conv_second))
    result_patch = results.reshape((total_slots,) + results.shape[2:])[flat_index]
    output = (gate[:, None, None, None] * result_patch.astype(jnp.float32)).astype(jnp.bfloat16)
    gate_grad = lax.optimization_barrier(jnp.sum(cotangent.astype(jnp.float32) * result_patch.astype(jnp.float32), axis=(1, 2, 3)))
    tiles_grad = tile_grads.reshape((total_slots,) + tile_grads.shape[2:])[flat_index]
    return (output, tiles_grad, first_grad, second_grad, gate_grad)
```

```python
import jax
import jax.numpy as jnp
from jax import lax
from jax.sharding import Mesh
from jax.sharding import PartitionSpec as P

SWAP = [(0, 3), (2, 1)]
SWAP_HOME = [(3, 0), (1, 2)]
LAYOUT = ("NHWC", "HWIO", "NHWC")


def as_sent(shard):

    def short(part):
        return part.astype(jnp.bfloat16) if part.dtype == jnp.float32 else part

    return jax.tree.map(short, shard)


def convolve(inputs, kernel):
    return lax.conv_general_dilated(
        inputs,
        kernel,
        (1, 1),
        "VALID",
        dimension_numbers=LAYOUT,
        preferred_element_type=jnp.float32,
    )


def transpose_conv(gradient, kernel):
    padded = jnp.pad(gradient, ((0, 0), (2, 2), (2, 2), (0, 0)))
    flipped = jnp.transpose(kernel[::-1, ::-1], (0, 1, 3, 2))
    return convolve(padded, flipped)


def kernel_grad(inputs, gradient):
    height_out = gradient.shape[1]
    width_out = gradient.shape[2]
    pieces = []
    for row_shift in range(3):
        for col_shift in range(3):
            window = inputs[
                :, row_shift : row_shift + height_out, col_shift : col_shift + width_out, :
            ]
            pieces.append(
                jnp.einsum("nijc,nijd->cd", window, gradient, preferred_element_type=jnp.float32)
            )
    stacked = jnp.stack(pieces)
    return stacked.reshape((3, 3) + stacked.shape[1:])


def silu_slope(pre_act):
    sigma_val = jax.nn.sigmoid(pre_act)
    return sigma_val * (1.0 + pre_act * (1.0 - sigma_val))


def flatten_two(values):
    return values.reshape((values.shape[0] * values.shape[1],) + values.shape[2:])


def unflatten_two(values, leading, items):
    return values.reshape((leading, items) + values.shape[1:])


def shards(tiles, route, gate, conv_first, conv_second, cotangent):
    halves = lax.axis_size("half")
    per_half = lax.axis_size("owner")
    cores = lax.axis_size("replica")
    half = lax.axis_index("half")
    core = lax.axis_index("replica")
    owners = halves * per_half
    patch_count = tiles.shape[0]
    capacity = max(2, (patch_count + owners - 1) // owners)
    onehot = (route[:, None] == jnp.arange(owners, dtype=jnp.int32)[None, :]).astype(jnp.int32)
    rank_within = jnp.cumsum(onehot, axis=0) - 1
    slot_index = jnp.sum(onehot * rank_within, axis=1)
    route_core = (route // per_half - half + halves) % halves
    target = ((route % per_half) * cores + route_core) * capacity + slot_index
    other_one, other_two = lax.ppermute((conv_first[0], conv_second[0]), ("half", "replica"), SWAP)
    kernel_one = jnp.where(core == 0, conv_first[0], other_one)
    kernel_two = jnp.where(core == 0, conv_second[0], other_two)
    gate_column = gate[:, None, None, None]
    scaled = (gate_column * cotangent.astype(jnp.float32)).astype(jnp.bfloat16)

    def to_slots(values):
        blank_slots = jnp.zeros((owners * capacity,) + values.shape[1:], values.dtype)
        filled = blank_slots.at[target].set(values)
        return filled.reshape((owners, capacity) + values.shape[1:])

    received = lax.all_to_all(to_slots(tiles), ("owner", "replica"), split_axis=0, concat_axis=0, tiled=True)
    leading = received.shape[0]
    items = received.shape[1]
    pre_act = convolve(flatten_two(received), kernel_one)
    hidden = jax.nn.silu(pre_act).astype(jnp.bfloat16)
    result = convolve(hidden, kernel_two).astype(jnp.bfloat16)
    pre_act, hidden, result = (
        unflatten_two(pre_act, leading, items),
        unflatten_two(hidden, leading, items),
        unflatten_two(result, leading, items),
    )
    back_result = lax.all_to_all(
        as_sent(result), ("owner", "replica"), split_axis=0, concat_axis=0, tiled=True
    ).astype(result.dtype)
    back_result, pre_act, hidden, received = (back_result, pre_act, hidden, received)
    grads_in = lax.all_to_all(to_slots(scaled), ("owner", "replica"), split_axis=0, concat_axis=0, tiled=True)
    leading = grads_in.shape[0]
    items = grads_in.shape[1]
    grad_hidden = transpose_conv(flatten_two(grads_in), kernel_two)
    grad_mid = (grad_hidden * silu_slope(flatten_two(pre_act))).astype(jnp.bfloat16)
    tile_grad = transpose_conv(grad_mid, kernel_one).astype(jnp.bfloat16)
    grad_mid, tile_grad = (
        unflatten_two(grad_mid, leading, items),
        unflatten_two(tile_grad, leading, items),
    )
    back_grad = lax.all_to_all(
        as_sent(tile_grad), ("owner", "replica"), split_axis=0, concat_axis=0, tiled=True
    ).astype(tile_grad.dtype)
    first_local = kernel_grad(flatten_two(received), flatten_two(grad_mid))
    second_local = kernel_grad(flatten_two(hidden), flatten_two(grads_in))

    def combine(local):
        away = lax.ppermute(local.astype(jnp.bfloat16), ("half", "replica"), SWAP_HOME)
        beside = lax.ppermute(local, "replica", [(0, 1)])
        own = jnp.where(core == 0, local, beside)
        passed = lax.ppermute(away, "replica", [(0, 1)])
        return own + jnp.where(core == 0, away, passed).astype(jnp.float32)

    first_grad = combine(first_local)
    second_grad = combine(second_local)
    result_patch = flatten_two(back_result)[target]
    tiles_grad = flatten_two(back_grad)[target]
    output = (gate_column * result_patch.astype(jnp.float32)).astype(jnp.bfloat16)
    gate_grad = jnp.sum(
        cotangent.astype(jnp.float32) * result_patch.astype(jnp.float32), axis=(1, 2, 3)
    )
    return (output, tiles_grad, first_grad[None], second_grad[None], gate_grad)


def solution(mesh):
    groups, experts, cores = (mesh.shape[a] for a in ("groups", "expert", "replica"))
    mesh = Mesh(
        mesh.devices.reshape(groups, cores, experts // cores, cores),
        ("groups", "half", "owner", "replica"),
    )
    placed = (
        P(("groups", "half", "owner", "replica"), None, None, None),
        P(("groups", "half", "owner", "replica")),
        P(("groups", "half", "owner", "replica")),
        P(("half", "owner"), None, None, None, None),
        P(("half", "owner"), None, None, None, None),
        P(("groups", "half", "owner", "replica"), None, None, None),
    )
    return jax.shard_map(
        shards,
        mesh=mesh,
        in_specs=placed,
        out_specs=(
            P(("groups", "half", "owner", "replica"), None, None, None),
            P(("groups", "half", "owner", "replica"), None, None, None),
            P(("groups", "half", "owner"), None, None, None, None),
            P(("groups", "half", "owner"), None, None, None, None),
            P(("groups", "half", "owner", "replica")),
        ),
        check_vma=False,
    )
```

```python
import functools

import jax
import jax.numpy as jnp
from jax import lax
from jax.experimental import pallas as pl
from jax.experimental.pallas import tpu as pltpu
from jax.sharding import Mesh
from jax.sharding import PartitionSpec as P

SWAP = [(0, 3), (2, 1)]
SWAP_HOME = [(3, 0), (1, 2)]
TAPS = 3
BLOCK = 8
SLOTS = 2
PARAMS = pltpu.CompilerParams(vmem_limit_bytes=40 * 1024 * 1024)


def dot(left, right):
    return jnp.dot(left, right, preferred_element_type=jnp.float32)


def iota(shape, dim):
    return lax.broadcasted_iota(jnp.int32, shape, dim)


def onto_rows(row):
    count = row.shape[1]
    eye = iota((count, count), 0) == iota((count, count), 1)
    return jnp.sum(jnp.where(eye, row, 0.0), axis=1, keepdims=True)


def slot_matrix(key, chunk, peers, cells_first):
    patches = key.shape[1]
    earlier = iota((patches, patches), 0) < iota((patches, patches), 1)
    same = onto_rows(key) == key
    rank = jnp.sum(jnp.where(same & earlier, 1.0, 0.0), axis=0, keepdims=True)
    code = key * 8.0 + rank
    columns = BLOCK * patches
    spread_row = iota((patches, columns), 0)
    spread_col = iota((patches, columns), 1)
    hit = (spread_col % patches) == spread_row if cells_first else (spread_col // BLOCK) == spread_row
    spread = jnp.where(hit, 1.0, 0.0)
    code_wide = jnp.sum(onto_rows(code) * spread, axis=0, keepdims=True)
    rows = peers * BLOCK * SLOTS
    row = iota((rows, columns), 0)
    col = iota((rows, columns), 1)
    row_code = (row // (BLOCK * SLOTS)) * 8 + (row % SLOTS + chunk * SLOTS)
    row_cell = (row // SLOTS) % BLOCK
    col_cell = col // patches if cells_first else col % BLOCK
    match = (row_code.astype(jnp.float32) == code_wide) & (row_cell == col_cell)
    return jnp.where(match, 1.0, 0.0).astype(jnp.bfloat16)


def pack_kernel(chunk, key_ref, gate_ref, tiles_ref, cot_ref, *out_refs):
    peers = len(out_refs)
    step = BLOCK * SLOTS
    key = key_ref[...]
    pick = slot_matrix(key, chunk, peers, True)
    blocks = tiles_ref.shape[0]

    def put(at, values):
        values = values.astype(jnp.bfloat16)
        for peer in range(peers):
            out_refs[peer][at : at + step, :] = values[peer * step : (peer + 1) * step, :]

    for block in range(blocks):
        put(block * step, dot(pick, tiles_ref[block]))
    pick = slot_matrix(key, chunk, peers, False)
    gate = onto_rows(gate_ref[...])[:, :, None]
    patches, rows, cols, channels = cot_ref.shape
    for i in range(rows):
        scaled = cot_ref[:, i, :, :].astype(jnp.float32) * gate
        scaled = scaled.reshape(patches * cols, channels).astype(jnp.bfloat16)
        put((blocks + i) * step, dot(pick, scaled))


def unpack_kernel(peers, key_ref, gate_ref, cot_ref, *refs):
    chunks = (len(refs) - 3) // peers
    msgs, (out_ref, tiles_ref, gate_grad_ref) = refs[: chunks * peers], refs[chunks * peers :]
    step = BLOCK * SLOTS
    key = key_ref[...]

    def spread(cells_first):
        picks = [slot_matrix(key, chunk, peers, cells_first) for chunk in range(chunks)]
        return jnp.concatenate(picks, axis=0).T

    def gather(block):
        return jnp.concatenate([m[block * step : (block + 1) * step, :] for m in msgs], axis=0)

    blocks = tiles_ref.shape[0]
    pick = spread(True)
    for block in range(blocks):
        tiles_ref[block] = dot(pick, gather(block)).astype(jnp.bfloat16)
    pick = spread(False)
    gate = onto_rows(gate_ref[...])[:, :, None]
    patches, rows, cols, channels = cot_ref.shape
    total = jnp.zeros((patches, cols, channels), jnp.float32)
    for i in range(rows):
        result = dot(pick, gather(blocks + i)).reshape(patches, cols, channels)
        out_ref[:, i, :, :] = (result * gate).astype(jnp.bfloat16)
        total = total + result * cot_ref[:, i, :, :].astype(jnp.float32)
    sums = jnp.sum(jnp.sum(total, axis=1), axis=1, keepdims=True)
    eye = iota((patches, patches), 0) == iota((patches, patches), 1)
    gate_grad_ref[...] = jnp.sum(jnp.where(eye, sums, 0.0), axis=0, keepdims=True)


def mix_matrix(peers, inverse):
    size = peers * BLOCK * SLOTS
    mixed, apart = (1, 0) if inverse else (0, 1)
    a = iota((size, size), mixed)
    b = iota((size, size), apart)
    cell_a, rest = a // (peers * SLOTS), a % (peers * SLOTS)
    from_b = (rest // SLOTS) * (BLOCK * SLOTS) + cell_a * SLOTS + rest % SLOTS
    return jnp.where(from_b == b, 1.0, 0.0).astype(jnp.bfloat16)


def expert_kernel(peers, side, *refs):
    msgs = refs[:peers]
    one_ref, two_ref, one_t_ref, two_t_ref = refs[peers : peers + 4]
    backs = refs[peers + 4 : 2 * peers + 4]
    x_ref, h_ref, g_ref, m_ref, slope_ref, t_ref = refs[2 * peers + 4 :]
    step = BLOCK * SLOTS
    wide = peers * SLOTS
    mid, out = side - 2, side - 4
    blocks = side * side // BLOCK
    size = BLOCK * wide

    def gather(block):
        return jnp.concatenate([m[block * step : (block + 1) * step, :] for m in msgs], axis=0)

    def window(ref, cols, row, col, count):
        at = (row * cols + col) * wide
        return ref[at : at + count * wide, :]

    mix = mix_matrix(peers, False)
    for block in range(blocks):
        x_ref[block * size : (block + 1) * size, :] = dot(mix, gather(block)).astype(jnp.bfloat16)
    for i in range(mid):
        lhs = jnp.concatenate(
            [window(x_ref, side, i + a, b, mid) for a in range(TAPS) for b in range(TAPS)], axis=1
        )
        pre = dot(lhs, one_ref[...])
        sigma = jax.nn.sigmoid(pre)
        rows = slice(i * mid * wide, (i + 1) * mid * wide)
        h_ref[rows, :] = (pre * sigma).astype(jnp.bfloat16)
        slope_ref[rows, :] = sigma * (1.0 + pre * (1.0 - sigma))

    apart = mix_matrix(peers, True)

    def put(block, values):
        values = dot(apart, values).astype(jnp.bfloat16)
        for peer in range(peers):
            backs[peer][block * step : (block + 1) * step, :] = values[peer * step : (peer + 1) * step, :]

    for i in range(out):
        lhs = jnp.concatenate(
            [window(h_ref, mid, i + a, b, out) for a in range(TAPS) for b in range(TAPS)], axis=1
        )
        put(blocks + i, dot(lhs, two_ref[...]).astype(jnp.bfloat16))

    blank = jnp.zeros((2 * wide, x_ref.shape[1]), jnp.bfloat16)
    for i in range(out):
        at = i * (out + 4) * wide
        g_ref[at : at + 2 * wide, :] = blank
        g_ref[at + 2 * wide : at + 2 * wide + size, :] = dot(mix, gather(blocks + i)).astype(jnp.bfloat16)
        g_ref[at + 2 * wide + size : at + 4 * wide + size, :] = blank

    def transposed(ref, kernel_ref, rows, i):
        taps = [a for a in range(TAPS) if 0 <= i - a < rows]
        lhs = jnp.concatenate(
            [window(ref, rows + 4, i - a, 2 - b, rows + 2) for a in taps for b in range(TAPS)], axis=1
        )
        per = TAPS * x_ref.shape[1]
        return dot(lhs, kernel_ref[taps[0] * per : (taps[-1] + 1) * per, :])

    for i in range(mid):
        at = i * (mid + 4) * wide
        grad_mid = transposed(g_ref, two_t_ref, out, i) * slope_ref[i * mid * wide : (i + 1) * mid * wide, :]
        m_ref[at : at + 2 * wide, :] = blank
        m_ref[at + 2 * wide : at + (mid + 2) * wide, :] = grad_mid.astype(jnp.bfloat16)
        m_ref[at + (mid + 2) * wide : at + (mid + 4) * wide, :] = blank
    for i in range(side):
        t_ref[i * side * wide : (i + 1) * side * wide, :] = transposed(m_ref, one_t_ref, mid, i).astype(
            jnp.bfloat16
        )
    for block in range(blocks):
        put(block, t_ref[block * size : (block + 1) * size, :])


def sums_kernel(side, wide, last, *refs):
    x_ref, h_ref, g_ref, m_ref = refs[:4]
    refs = refs[4:]
    before = None
    if last:
        before, refs = refs[:2], refs[2:]
    mid, out = side - 2, side - 4

    def one(in_ref, cols, grad_ref, rows, k):
        grads = [
            grad_ref[(i * (rows + 4) + 2) * wide : (i * (rows + 4) + 2 + rows) * wide, :] for i in range(rows)
        ]
        grad_t = jnp.concatenate(grads, axis=0).T
        for tap in range(TAPS * TAPS):
            a, b = divmod(tap, TAPS)
            window = jnp.concatenate(
                [
                    in_ref[((i + a) * cols + b) * wide : ((i + a) * cols + b + rows) * wide, :]
                    for i in range(rows)
                ],
                axis=0,
            )
            total = dot(grad_t, window)
            if last:
                total = (total + before[k][tap]).T
                refs[2 + k][tap] = total.astype(jnp.bfloat16)
            refs[k][tap] = total

    one(h_ref, mid, g_ref, out, 1)
    one(x_ref, side, m_ref, mid, 0)


def shards(tiles, route, gate, conv_first, conv_second, cotangent):
    halves = lax.axis_size("half")
    per_half = lax.axis_size("owner")
    cores = lax.axis_size("replica")
    half = lax.axis_index("half")
    core = lax.axis_index("replica")
    me = lax.axis_index("owner") * cores + core
    peers = per_half * cores
    patches, side, _, channels = tiles.shape
    out_side = cotangent.shape[1]
    capacity = max(2, (patches + peers - 1) // peers)
    chunks = capacity // SLOTS
    blocks = side * side // BLOCK
    message = (side * side + out_side * out_side) * SLOTS
    wide = peers * SLOTS

    other_one, other_two = (
        lax.ppermute(k[0], ("half", "replica"), SWAP) for k in (conv_first, conv_second)
    )
    route_core = (route // per_half - half + halves) % halves
    key = ((((route % per_half) * cores + route_core) ^ me).astype(jnp.float32))[None, :]
    gate_row = gate[None, :]
    tiles_rows = jnp.transpose(tiles, (1, 2, 0, 3)).reshape(blocks, BLOCK * patches, channels)

    bf16 = functools.partial(jax.ShapeDtypeStruct, dtype=jnp.bfloat16)
    f32 = functools.partial(jax.ShapeDtypeStruct, dtype=jnp.float32)

    def exchange(messages):
        got = [messages[0]]
        for mask in range(1, peers):
            pairs = [(i, i ^ mask) for i in range(peers)]
            got.append(lax.ppermute(messages[mask], ("owner", "replica"), pairs))
        return got

    def pack(chunk):
        return pl.pallas_call(
            functools.partial(pack_kernel, chunk),
            out_shape=[bf16((message, channels))] * peers,
            compiler_params=PARAMS,
            name="pack",
        )(key, gate_row, tiles_rows, cotangent)

    arrived = [exchange(pack(chunk)) for chunk in range(chunks)]

    kernel_one = jnp.where(core == 0, conv_first[0], other_one)
    kernel_two = jnp.where(core == 0, conv_second[0], other_two)
    flat = (TAPS * TAPS * channels, channels)
    weights = (
        kernel_one.reshape(flat),
        kernel_two.reshape(flat),
        jnp.swapaxes(kernel_one, 2, 3).reshape(flat),
        jnp.swapaxes(kernel_two, 2, 3).reshape(flat),
    )
    mid = side - 2
    kept = [
        bf16((side * side * wide, channels)),
        bf16((mid * mid * wide, channels)),
        bf16((out_side * side * wide, channels)),
        bf16((mid * (mid + 4) * wide, channels)),
    ]

    def expert(messages):
        result = pl.pallas_call(
            functools.partial(expert_kernel, peers, side),
            out_shape=[bf16((message, channels))] * peers + kept,
            scratch_shapes=[
                pltpu.VMEM((mid * mid * wide, channels), jnp.float32),
                pltpu.VMEM((side * side * wide, channels), jnp.bfloat16),
            ],
            compiler_params=PARAMS,
            name="expert",
        )(*messages, *weights)
        return result[:peers], result[peers:]

    def sums(held, before):
        last = before is not None or chunks == 1
        shape = (TAPS * TAPS, channels, channels)
        return pl.pallas_call(
            functools.partial(sums_kernel, side, wide, before is not None),
            out_shape=[f32(shape)] * 2 + ([bf16(shape)] * 2 if before is not None else []),
            compiler_params=PARAMS,
            name="sums",
        )(*held, *(before or []))

    backs, total = [], None
    for messages in arrived:
        back, held = expert(messages)
        backs.append(exchange(back))
        if total is None:
            shape = (TAPS * TAPS, channels, channels)
            total = [jnp.zeros(shape, jnp.float32)] * 2 if chunks == 1 else None
        total = sums(held, total)

    def combine(local, short):
        away = lax.ppermute(short, ("half", "replica"), SWAP_HOME)
        beside = lax.ppermute(local, "replica", [(0, 1)])
        own = jnp.where(core == 0, local, beside)
        passed = lax.ppermute(away, "replica", [(0, 1)])
        total = own + jnp.where(core == 0, away, passed).astype(jnp.float32)
        return total.reshape((1, TAPS, TAPS) + total.shape[1:])

    first_grad = combine(total[0], total[2])
    second_grad = combine(total[1], total[3])
    output, tiles_out, gate_grad = pl.pallas_call(
        functools.partial(unpack_kernel, peers),
        out_shape=[
            bf16(cotangent.shape),
            bf16(tiles_rows.shape),
            f32((1, patches)),
        ],
        compiler_params=PARAMS,
        name="unpack",
    )(key, gate_row, cotangent, *[m for back in backs for m in back])
    tiles_grad = jnp.transpose(tiles_out.reshape(side, side, patches, channels), (2, 0, 1, 3))
    return (output, tiles_grad, first_grad, second_grad, gate_grad[0])


def solution(mesh):
    groups, experts, cores = (mesh.shape[a] for a in ("groups", "expert", "replica"))
    mesh = Mesh(
        mesh.devices.reshape(groups, cores, experts // cores, cores),
        ("groups", "half", "owner", "replica"),
    )
    every = ("groups", "half", "owner", "replica")
    placed = (
        P(every, None, None, None),
        P(every),
        P(every),
        P(("half", "owner"), None, None, None, None),
        P(("half", "owner"), None, None, None, None),
        P(every, None, None, None),
    )
    return jax.shard_map(
        shards,
        mesh=mesh,
        in_specs=placed,
        out_specs=(
            P(every, None, None, None),
            P(every, None, None, None),
            P(("groups", "half", "owner"), None, None, None, None),
            P(("groups", "half", "owner"), None, None, None, None),
            P(every),
        ),
        check_vma=False,
    )
```

```python
import functools

import jax
import jax.numpy as jnp
from jax import lax
from jax.experimental import pallas as pl
from jax.experimental.pallas import tpu as pltpu
from jax.sharding import Mesh
from jax.sharding import PartitionSpec as P

SWAP = [(0, 3), (2, 1)]
SWAP_HOME = [(1, 3), (3, 1)]
TAPS = 3
BLOCK = 8
PARAMS = pltpu.CompilerParams(vmem_limit_bytes=40 * 1024 * 1024)


def dot(left, right):
    return jnp.dot(left, right, preferred_element_type=jnp.float32)


def iota(shape, dim):
    return lax.broadcasted_iota(jnp.int32, shape, dim)


def onto_rows(row):
    count = row.shape[1]
    eye = iota((count, count), 0) == iota((count, count), 1)
    return jnp.sum(jnp.where(eye, row, 0.0), axis=1, keepdims=True)


def slot_matrix(key, slots, peers, cells_first):
    patches = key.shape[1]
    earlier = iota((patches, patches), 0) < iota((patches, patches), 1)
    same = onto_rows(key) == key
    rank = jnp.sum(jnp.where(same & earlier, 1.0, 0.0), axis=0, keepdims=True)
    code = key * 8.0 + rank
    columns = BLOCK * patches
    spread_row = iota((patches, columns), 0)
    spread_col = iota((patches, columns), 1)
    hit = (spread_col % patches) == spread_row if cells_first else (spread_col // BLOCK) == spread_row
    spread = jnp.where(hit, 1.0, 0.0)
    code_wide = jnp.sum(onto_rows(code) * spread, axis=0, keepdims=True)
    rows = peers * BLOCK * slots
    row = iota((rows, columns), 0)
    col = iota((rows, columns), 1)
    row_code = (row // (BLOCK * slots)) * 8 + row % slots
    row_cell = (row // slots) % BLOCK
    col_cell = col // patches if cells_first else col % BLOCK
    match = (row_code.astype(jnp.float32) == code_wide) & (row_cell == col_cell)
    return jnp.where(match, 1.0, 0.0).astype(jnp.bfloat16)


def pack_kernel(slots, key_ref, gate_ref, tiles_ref, cot_ref, *out_refs):
    peers = len(out_refs)
    step = BLOCK * slots
    key = key_ref[...]
    pick = slot_matrix(key, slots, peers, True)
    blocks = tiles_ref.shape[0]

    def put(at, values):
        values = values.astype(jnp.bfloat16)
        for peer in range(peers):
            out_refs[peer][at : at + step, :] = values[peer * step : (peer + 1) * step, :]

    for block in range(blocks):
        put(block * step, dot(pick, tiles_ref[block]))
    pick = slot_matrix(key, slots, peers, False)
    gate = onto_rows(gate_ref[...])[:, :, None]
    patches, rows, cols, channels = cot_ref.shape
    for i in range(rows):
        scaled = cot_ref[:, i, :, :].astype(jnp.float32) * gate
        scaled = scaled.reshape(patches * cols, channels).astype(jnp.bfloat16)
        put((blocks + i) * step, dot(pick, scaled))


def unpack_kernel(slots, key_ref, gate_ref, cot_ref, *refs):
    msgs, (out_ref, tiles_ref, gate_grad_ref) = refs[:-3], refs[-3:]
    peers = len(msgs)
    step = BLOCK * slots
    key = key_ref[...]

    def gather(block):
        return jnp.concatenate([m[block * step : (block + 1) * step, :] for m in msgs], axis=0)

    blocks = tiles_ref.shape[0]
    pick = slot_matrix(key, slots, peers, True).T
    for block in range(blocks):
        tiles_ref[block] = dot(pick, gather(block)).astype(jnp.bfloat16)
    pick = slot_matrix(key, slots, peers, False).T
    gate = onto_rows(gate_ref[...])[:, :, None]
    patches, rows, cols, channels = cot_ref.shape
    total = jnp.zeros((patches, cols, channels), jnp.float32)
    for i in range(rows):
        result = dot(pick, gather(blocks + i)).reshape(patches, cols, channels)
        out_ref[:, i, :, :] = (result * gate).astype(jnp.bfloat16)
        total = total + result * cot_ref[:, i, :, :].astype(jnp.float32)
    sums = jnp.sum(jnp.sum(total, axis=1), axis=1, keepdims=True)
    eye = iota((patches, patches), 0) == iota((patches, patches), 1)
    gate_grad_ref[...] = jnp.sum(jnp.where(eye, sums, 0.0), axis=0, keepdims=True)


def mix_matrix(peers, slots, inverse):
    size = peers * BLOCK * slots
    mixed, apart = (1, 0) if inverse else (0, 1)
    a = iota((size, size), mixed)
    b = iota((size, size), apart)
    cell_a, rest = a // (peers * slots), a % (peers * slots)
    from_b = (rest // slots) * (BLOCK * slots) + cell_a * slots + rest % slots
    return jnp.where(from_b == b, 1.0, 0.0).astype(jnp.bfloat16)


def expert_kernel(peers, slots, side, *refs):
    msgs = refs[:peers]
    one_ref, two_ref, one_t_ref, two_t_ref = refs[peers : peers + 4]
    backs = refs[-peers - 6 : -6]
    x_ref, h_ref, g_ref, m_ref, slope_ref, t_ref = refs[-6:]
    step = BLOCK * slots
    wide = peers * slots
    mid, out = side - 2, side - 4
    blocks = side * side // BLOCK
    size = BLOCK * wide

    def gather(block):
        return jnp.concatenate([m[block * step : (block + 1) * step, :] for m in msgs], axis=0)

    def window(ref, cols, row, col, count):
        at = (row * cols + col) * wide
        return ref[at : at + count * wide, :]

    mix = mix_matrix(peers, slots, False)
    for block in range(blocks):
        x_ref[block * size : (block + 1) * size, :] = dot(mix, gather(block)).astype(jnp.bfloat16)
    for i in range(mid):
        lhs = jnp.concatenate(
            [window(x_ref, side, i + a, b, mid) for a in range(TAPS) for b in range(TAPS)], axis=1
        )
        pre = dot(lhs, one_ref[...])
        sigma = jax.nn.sigmoid(pre)
        rows = slice(i * mid * wide, (i + 1) * mid * wide)
        h_ref[rows, :] = (pre * sigma).astype(jnp.bfloat16)
        slope_ref[rows, :] = sigma * (1.0 + pre * (1.0 - sigma))

    apart = mix_matrix(peers, slots, True)

    def put(block, values):
        values = dot(apart, values).astype(jnp.bfloat16)
        for peer in range(peers):
            backs[peer][block * step : (block + 1) * step, :] = values[peer * step : (peer + 1) * step, :]

    for i in range(out):
        lhs = jnp.concatenate(
            [window(h_ref, mid, i + a, b, out) for a in range(TAPS) for b in range(TAPS)], axis=1
        )
        put(blocks + i, dot(lhs, two_ref[...]).astype(jnp.bfloat16))

    blank = jnp.zeros((2 * wide, x_ref.shape[1]), jnp.bfloat16)
    for i in range(out):
        at = i * (out + 4) * wide
        g_ref[at : at + 2 * wide, :] = blank
        g_ref[at + 2 * wide : at + 2 * wide + size, :] = dot(mix, gather(blocks + i)).astype(jnp.bfloat16)
        g_ref[at + 2 * wide + size : at + 4 * wide + size, :] = blank

    def transposed(ref, kernel_ref, rows, i):
        taps = [a for a in range(TAPS) if 0 <= i - a < rows]
        lhs = jnp.concatenate(
            [window(ref, rows + 4, i - a, 2 - b, rows + 2) for a in taps for b in range(TAPS)], axis=1
        )
        per = TAPS * x_ref.shape[1]
        return dot(lhs, kernel_ref[taps[0] * per : (taps[-1] + 1) * per, :])

    for i in range(mid):
        at = i * (mid + 4) * wide
        grad_mid = transposed(g_ref, two_t_ref, out, i) * slope_ref[i * mid * wide : (i + 1) * mid * wide, :]
        m_ref[at : at + 2 * wide, :] = blank
        m_ref[at + 2 * wide : at + (mid + 2) * wide, :] = grad_mid.astype(jnp.bfloat16)
        m_ref[at + (mid + 2) * wide : at + (mid + 4) * wide, :] = blank
    for i in range(side):
        t_ref[i * side * wide : (i + 1) * side * wide, :] = transposed(m_ref, one_t_ref, mid, i).astype(
            jnp.bfloat16
        )
    for block in range(blocks):
        put(block, t_ref[block * size : (block + 1) * size, :])


def sums_kernel(side, wide, first, last, *refs):
    x_ref, h_ref, g_ref, m_ref = refs[:4]
    before_ref = None if first else refs[4]
    out_ref = refs[-1]
    mid, out = side - 2, side - 4

    def one(in_ref, cols, grad_ref, rows, k):
        grads = [
            grad_ref[(i * (rows + 4) + 2) * wide : (i * (rows + 4) + 2 + rows) * wide, :] for i in range(rows)
        ]
        grad_t = jnp.concatenate(grads, axis=0).T
        for tap in range(TAPS * TAPS):
            a, b = divmod(tap, TAPS)
            window = jnp.concatenate(
                [
                    in_ref[((i + a) * cols + b) * wide : ((i + a) * cols + b + rows) * wide, :]
                    for i in range(rows)
                ],
                axis=0,
            )
            at = k * TAPS * TAPS + tap
            total = dot(grad_t, window)
            if not first:
                total = total + before_ref[at]
            out_ref[at] = total.T.astype(jnp.bfloat16) if last else total

    one(h_ref, mid, g_ref, out, 1)
    one(x_ref, side, m_ref, mid, 0)


def shards(tiles, route, gate, conv_first, conv_second, cotangent):
    halves = lax.axis_size("half")
    per_half = lax.axis_size("owner")
    cores = lax.axis_size("replica")
    half = lax.axis_index("half")
    core = lax.axis_index("replica")
    me = lax.axis_index("owner") * cores + core
    peers = per_half * cores
    patches, side, _, channels = tiles.shape
    out_side = cotangent.shape[1]
    slots = max(2, (patches + peers - 1) // peers)
    blocks = side * side // BLOCK
    message = (side * side + out_side * out_side) * slots
    order = sorted(range(peers), key=lambda mask: (mask >= cores, -(mask // cores).bit_count(), mask % cores, mask))
    chunks = (order[: peers // 2], order[peers // 2 :])
    part = peers // 2
    wide = part * slots

    other_one, other_two = (
        lax.ppermute(k[0], ("half", "replica"), SWAP) for k in (conv_first, conv_second)
    )
    route_core = (route // per_half - half + halves) % halves
    key = ((((route % per_half) * cores + route_core) ^ me).astype(jnp.float32))[None, :]
    gate_row = gate[None, :]
    tiles_rows = jnp.transpose(tiles, (1, 2, 0, 3)).reshape(blocks, BLOCK * patches, channels)

    bf16 = functools.partial(jax.ShapeDtypeStruct, dtype=jnp.bfloat16)
    f32 = functools.partial(jax.ShapeDtypeStruct, dtype=jnp.float32)

    def exchange(mask, message, after=None):
        if mask == 0:
            return message
        if after is not None:
            message, _ = lax.optimization_barrier((message, after))
        return lax.ppermute(message, ("owner", "replica"), [(i, i ^ mask) for i in range(peers)])

    packed = pl.pallas_call(
        functools.partial(pack_kernel, slots),
        out_shape=[bf16((message, channels))] * peers,
        compiler_params=PARAMS,
        name="pack",
    )(key, gate_row, tiles_rows, cotangent)
    arrived = [[exchange(mask, packed[mask]) for mask in chunks[0]]]
    leading = [None, None] + arrived[0][2:]
    arrived.append([exchange(mask, packed[mask], leading[i % len(leading)]) for i, mask in enumerate(chunks[1])])

    kernel_one = jnp.where(core == 0, conv_first[0], other_one)
    kernel_two = jnp.where(core == 0, conv_second[0], other_two)
    flat = (TAPS * TAPS * channels, channels)
    weights = (
        kernel_one.reshape(flat),
        kernel_two.reshape(flat),
        jnp.swapaxes(kernel_one, 2, 3).reshape(flat),
        jnp.swapaxes(kernel_two, 2, 3).reshape(flat),
    )
    mid = side - 2

    def cost(cells):
        flops = int(cells * wide * TAPS * TAPS * channels * channels * 8)
        return pl.CostEstimate(flops=flops, bytes_accessed=flops // 500, transcendentals=0)

    kept = [
        bf16((side * side * wide, channels)),
        bf16((mid * mid * wide, channels)),
        bf16((out_side * side * wide, channels)),
        bf16((mid * (mid + 4) * wide, channels)),
    ]

    def expert(messages, after):
        specs = [pl.BlockSpec()] * (len(messages) + len(weights))
        specs = specs + [pl.BlockSpec(memory_space=pl.ANY)] * len(after)
        result = pl.pallas_call(
            functools.partial(expert_kernel, part, slots, side),
            in_specs=specs,
            out_shape=[bf16((message, channels))] * part + kept,
            scratch_shapes=[
                pltpu.VMEM((mid * mid * wide, channels), jnp.float32),
                pltpu.VMEM((side * side * wide, channels), jnp.bfloat16),
            ],
            compiler_params=PARAMS,
            cost_estimate=cost(2.0 * (2 * mid * mid + out_side * out_side + side * side)),
            name="expert",
        )(*messages, *weights, *after)
        return result[:part], result[part:]

    def sums(held, before, after, last):
        specs = [pl.BlockSpec()] * (len(held) + len(before))
        specs = specs + [pl.BlockSpec(memory_space=pl.ANY)] * len(after)
        shape = (2 * TAPS * TAPS, channels, channels)
        return pl.pallas_call(
            functools.partial(sums_kernel, side, wide, not before, last),
            in_specs=specs,
            out_shape=bf16(shape) if last else f32(shape),
            compiler_params=PARAMS,
            cost_estimate=cost(2.0 * (mid * mid + out_side * out_side)),
            name="sums",
        )(*held, *before, *after)

    backs, total = {}, []
    for chunk, messages in zip(chunks, arrived):
        back, held = expert(messages, total)
        after = [backs[mask] for mask in backs if mask]
        for mask, returned in zip(chunk, back):
            backs[mask] = exchange(mask, returned)
        total = [sums(held, total, after, chunk is chunks[-1])]

    away = lax.ppermute(total[0], ("half", "replica"), SWAP_HOME)
    away, _ = lax.optimization_barrier((away, [backs[mask] for mask in chunks[1]]))
    away = jnp.where(core == 0, total[0], away)
    beside = lax.ppermute(away, "replica", [(0, 1), (1, 0)])
    grads = away.astype(jnp.float32) + beside.astype(jnp.float32)
    first_grad, second_grad = grads.reshape((2, 1, TAPS, TAPS, channels, channels))
    output, tiles_out, gate_grad = pl.pallas_call(
        functools.partial(unpack_kernel, slots),
        out_shape=[
            bf16(cotangent.shape),
            bf16(tiles_rows.shape),
            f32((1, patches)),
        ],
        compiler_params=PARAMS,
        name="unpack",
    )(key, gate_row, cotangent, *[backs[mask] for mask in range(peers)])
    tiles_grad = jnp.transpose(tiles_out.reshape(side, side, patches, channels), (2, 0, 1, 3))
    return (output, tiles_grad, first_grad, second_grad, gate_grad[0])


def solution(mesh):
    groups, experts, cores = (mesh.shape[a] for a in ("groups", "expert", "replica"))
    mesh = Mesh(
        mesh.devices.reshape(groups, cores, experts // cores, cores),
        ("groups", "half", "owner", "replica"),
    )
    every = ("groups", "half", "owner", "replica")
    placed = (
        P(every, None, None, None),
        P(every),
        P(every),
        P(("half", "owner"), None, None, None, None),
        P(("half", "owner"), None, None, None, None),
        P(every, None, None, None),
    )
    return jax.shard_map(
        shards,
        mesh=mesh,
        in_specs=placed,
        out_specs=(
            P(every, None, None, None),
            P(every, None, None, None),
            P(("groups", "half", "owner"), None, None, None, None),
            P(("groups", "half", "owner"), None, None, None, None),
            P(every),
        ),
        check_vma=False,
    )
```

```python
import functools

import jax
import jax.numpy as jnp
from jax import lax
from jax.experimental import pallas as pl
from jax.experimental.pallas import tpu as pltpu
from jax.sharding import Mesh
from jax.sharding import PartitionSpec as P

SWAP = [(0, 3), (2, 1)]
SWAP_HOME = [(1, 3), (3, 1)]
TAPS = 3
BLOCK = 8
PARAMS = pltpu.CompilerParams(vmem_limit_bytes=40 * 1024 * 1024)


def dot(left, right):
    return jnp.dot(left, right, preferred_element_type=jnp.float32)


def iota(shape, dim):
    return lax.broadcasted_iota(jnp.int32, shape, dim)


def onto_rows(row):
    count = row.shape[1]
    eye = iota((count, count), 0) == iota((count, count), 1)
    return jnp.sum(jnp.where(eye, row, 0.0), axis=1, keepdims=True)


def slot_matrix(key, slots, peers, cells_first):
    patches = key.shape[1]
    earlier = iota((patches, patches), 0) < iota((patches, patches), 1)
    same = onto_rows(key) == key
    rank = jnp.sum(jnp.where(same & earlier, 1.0, 0.0), axis=0, keepdims=True)
    code = key * 8.0 + rank
    columns = BLOCK * patches
    spread_row = iota((patches, columns), 0)
    spread_col = iota((patches, columns), 1)
    hit = (spread_col % patches) == spread_row if cells_first else (spread_col // BLOCK) == spread_row
    spread = jnp.where(hit, 1.0, 0.0)
    code_wide = jnp.sum(onto_rows(code) * spread, axis=0, keepdims=True)
    rows = peers * BLOCK * slots
    row = iota((rows, columns), 0)
    col = iota((rows, columns), 1)
    row_code = (row // (BLOCK * slots)) * 8 + row % slots
    row_cell = (row // slots) % BLOCK
    col_cell = col // patches if cells_first else col % BLOCK
    match = (row_code.astype(jnp.float32) == code_wide) & (row_cell == col_cell)
    return jnp.where(match, 1.0, 0.0).astype(jnp.bfloat16)


def pack_kernel(slots, key_ref, gate_ref, tiles_ref, cot_ref, *out_refs):
    peers = len(out_refs)
    step = BLOCK * slots
    key = key_ref[...]
    pick = slot_matrix(key, slots, peers, True)
    blocks = tiles_ref.shape[0]

    def put(at, values):
        values = values.astype(jnp.bfloat16)
        for peer in range(peers):
            out_refs[peer][at : at + step, :] = values[peer * step : (peer + 1) * step, :]

    for block in range(blocks):
        put(block * step, dot(pick, tiles_ref[block]))
    pick = slot_matrix(key, slots, peers, False)
    gate = onto_rows(gate_ref[...])[:, :, None]
    patches, rows, cols, channels = cot_ref.shape
    for i in range(rows):
        scaled = cot_ref[:, i, :, :].astype(jnp.float32) * gate
        scaled = scaled.reshape(patches * cols, channels).astype(jnp.bfloat16)
        put((blocks + i) * step, dot(pick, scaled))


def unpack_kernel(slots, queue, key_ref, gate_ref, cot_ref, *refs):
    msgs, (out_ref, tiles_ref, gate_grad_ref) = refs[:-3], refs[-3:]
    msgs = [msgs[queue.index(peer)] for peer in range(len(msgs))]
    peers = len(msgs)
    step = BLOCK * slots
    key = key_ref[...]

    def gather(block):
        return jnp.concatenate([m[block * step : (block + 1) * step, :] for m in msgs], axis=0)

    blocks = tiles_ref.shape[0]
    pick = slot_matrix(key, slots, peers, True).T
    for block in range(blocks):
        tiles_ref[block] = dot(pick, gather(block)).astype(jnp.bfloat16)
    pick = slot_matrix(key, slots, peers, False).T
    gate = onto_rows(gate_ref[...])[:, :, None]
    patches, rows, cols, channels = cot_ref.shape
    total = jnp.zeros((patches, cols, channels), jnp.float32)
    for i in range(rows):
        result = dot(pick, gather(blocks + i)).reshape(patches, cols, channels)
        out_ref[:, i, :, :] = (result * gate).astype(jnp.bfloat16)
        total = total + result * cot_ref[:, i, :, :].astype(jnp.float32)
    sums = jnp.sum(jnp.sum(total, axis=1), axis=1, keepdims=True)
    eye = iota((patches, patches), 0) == iota((patches, patches), 1)
    gate_grad_ref[...] = jnp.sum(jnp.where(eye, sums, 0.0), axis=0, keepdims=True)


def mix_matrix(peers, slots, inverse):
    size = peers * BLOCK * slots
    mixed, apart = (1, 0) if inverse else (0, 1)
    a = iota((size, size), mixed)
    b = iota((size, size), apart)
    cell_a, rest = a // (peers * slots), a % (peers * slots)
    from_b = (rest // slots) * (BLOCK * slots) + cell_a * slots + rest % slots
    return jnp.where(from_b == b, 1.0, 0.0).astype(jnp.bfloat16)


def expert_kernel(peers, slots, side, earlier, last, *refs):
    msgs = refs[:peers]
    one_ref, two_ref, one_t_ref, two_t_ref = refs[peers : peers + 4]
    held = [refs[peers + 4 + 4 * k : peers + 8 + 4 * k] for k in range(earlier)]
    outs = refs[peers + 4 + 4 * earlier :]
    backs = outs[:peers]
    sums_ref = outs[peers] if last else None
    x_ref, h_ref, g_ref, m_ref, slope_ref, t_ref = outs[-6:]
    step = BLOCK * slots
    wide = peers * slots
    mid, out = side - 2, side - 4
    blocks = side * side // BLOCK
    size = BLOCK * wide

    def gather(block):
        return jnp.concatenate([m[block * step : (block + 1) * step, :] for m in msgs], axis=0)

    def window(ref, cols, row, col, count):
        at = (row * cols + col) * wide
        return ref[at : at + count * wide, :]

    mix = mix_matrix(peers, slots, False)
    for block in range(blocks):
        x_ref[block * size : (block + 1) * size, :] = dot(mix, gather(block)).astype(jnp.bfloat16)
    for i in range(mid):
        lhs = jnp.concatenate(
            [window(x_ref, side, i + a, b, mid) for a in range(TAPS) for b in range(TAPS)], axis=1
        )
        pre = dot(lhs, one_ref[...])
        sigma = jax.nn.sigmoid(pre)
        rows = slice(i * mid * wide, (i + 1) * mid * wide)
        h_ref[rows, :] = (pre * sigma).astype(jnp.bfloat16)
        slope_ref[rows, :] = sigma * (1.0 + pre * (1.0 - sigma))

    apart = mix_matrix(peers, slots, True)

    def put(block, values):
        values = dot(apart, values).astype(jnp.bfloat16)
        for peer in range(peers):
            backs[peer][block * step : (block + 1) * step, :] = values[peer * step : (peer + 1) * step, :]

    for i in range(out):
        lhs = jnp.concatenate(
            [window(h_ref, mid, i + a, b, out) for a in range(TAPS) for b in range(TAPS)], axis=1
        )
        put(blocks + i, dot(lhs, two_ref[...]).astype(jnp.bfloat16))

    blank = jnp.zeros((2 * wide, x_ref.shape[1]), jnp.bfloat16)
    for i in range(out):
        at = i * (out + 4) * wide
        g_ref[at : at + 2 * wide, :] = blank
        g_ref[at + 2 * wide : at + 2 * wide + size, :] = dot(mix, gather(blocks + i)).astype(jnp.bfloat16)
        g_ref[at + 2 * wide + size : at + 4 * wide + size, :] = blank

    def transposed(ref, kernel_ref, rows, i):
        taps = [a for a in range(TAPS) if 0 <= i - a < rows]
        lhs = jnp.concatenate(
            [window(ref, rows + 4, i - a, 2 - b, rows + 2) for a in taps for b in range(TAPS)], axis=1
        )
        per = TAPS * x_ref.shape[1]
        return dot(lhs, kernel_ref[taps[0] * per : (taps[-1] + 1) * per, :])

    for i in range(mid):
        at = i * (mid + 4) * wide
        grad_mid = transposed(g_ref, two_t_ref, out, i) * slope_ref[i * mid * wide : (i + 1) * mid * wide, :]
        m_ref[at : at + 2 * wide, :] = blank
        m_ref[at + 2 * wide : at + (mid + 2) * wide, :] = grad_mid.astype(jnp.bfloat16)
        m_ref[at + (mid + 2) * wide : at + (mid + 4) * wide, :] = blank
    for i in range(side):
        t_ref[i * side * wide : (i + 1) * side * wide, :] = transposed(m_ref, one_t_ref, mid, i).astype(
            jnp.bfloat16
        )
    for block in range(blocks):
        put(block, t_ref[block * size : (block + 1) * size, :])


    if last:
        held = held + [(x_ref, h_ref, g_ref, m_ref)]
        kernel_sums([k[0] for k in held], side, [k[3] for k in held], mid, wide, sums_ref, 0)
        kernel_sums([k[1] for k in held], mid, [k[2] for k in held], out, wide, sums_ref, 1)


def kernel_sums(in_refs, cols, grad_refs, rows, wide, sums_ref, k):
    taps = TAPS * TAPS

    def window(ref, tap):
        a, b = divmod(tap, TAPS)
        starts = [((i + a) * cols + b) * wide for i in range(rows)]
        return [ref[at : at + rows * wide, :] for at in starts]

    grads = []
    for ref in grad_refs:
        starts = [(i * (rows + 4) + 2) * wide for i in range(rows)]
        grads = grads + [ref[at : at + rows * wide, :] for at in starts]
    grad_t = jnp.concatenate(grads, axis=0).T
    for first in range(0, taps, 2):
        pair = range(first, min(first + 2, taps))
        windows = [jnp.concatenate([w for ref in in_refs for w in window(ref, tap)], axis=0) for tap in pair]
        total = dot(grad_t, jnp.concatenate(windows, axis=1))
        channels = windows[0].shape[1]
        for j, tap in enumerate(pair):
            part = total[:, j * channels : (j + 1) * channels]
            sums_ref[k * taps + tap] = part.T.astype(jnp.bfloat16)


def shards(tiles, route, gate, conv_first, conv_second, cotangent):
    halves = lax.axis_size("half")
    per_half = lax.axis_size("owner")
    cores = lax.axis_size("replica")
    half = lax.axis_index("half")
    core = lax.axis_index("replica")
    me = lax.axis_index("owner") * cores + core
    peers = per_half * cores
    patches, side, _, channels = tiles.shape
    out_side = cotangent.shape[1]
    slots = max(2, (patches + peers - 1) // peers)
    blocks = side * side // BLOCK
    message = (side * side + out_side * out_side) * slots
    order = sorted(range(peers), key=lambda mask: (mask >= cores, -(mask // cores).bit_count(), mask % cores, mask))
    chunks = (order[: peers // 2], order[peers // 2 :])
    part = peers // 2
    wide = part * slots

    other_one, other_two = (
        lax.ppermute(k[0], ("half", "replica"), SWAP) for k in (conv_first, conv_second)
    )
    route_core = (route // per_half - half + halves) % halves
    key = ((((route % per_half) * cores + route_core) ^ me).astype(jnp.float32))[None, :]
    gate_row = gate[None, :]
    tiles_rows = jnp.transpose(tiles, (1, 2, 0, 3)).reshape(blocks, BLOCK * patches, channels)

    bf16 = functools.partial(jax.ShapeDtypeStruct, dtype=jnp.bfloat16)
    f32 = functools.partial(jax.ShapeDtypeStruct, dtype=jnp.float32)

    def exchange(mask, message, after=None):
        if mask == 0:
            return message
        if after is not None:
            message, _ = lax.optimization_barrier((message, after))
        return lax.ppermute(message, ("owner", "replica"), [(i, i ^ mask) for i in range(peers)])

    packed = pl.pallas_call(
        functools.partial(pack_kernel, slots),
        out_shape=[bf16((message, channels))] * peers,
        compiler_params=PARAMS,
        name="pack",
    )(key, gate_row, tiles_rows, cotangent)
    nearer = sorted(chunks[1], key=lambda mask: (mask % cores, -mask))
    queue = [mask for mask in chunks[0] if mask >= cores] + order[1:cores] + nearer
    got = {0: packed[0]}
    for i, mask in enumerate(queue):
        got[mask] = exchange(mask, packed[mask], got[queue[i - 4]] if i >= 4 else None)
    arrived = [[got[mask] for mask in chunk] for chunk in chunks]

    kernel_one = jnp.where(core == 0, conv_first[0], other_one)
    kernel_two = jnp.where(core == 0, conv_second[0], other_two)
    flat = (TAPS * TAPS * channels, channels)
    weights = (
        kernel_one.reshape(flat),
        kernel_two.reshape(flat),
        jnp.swapaxes(kernel_one, 2, 3).reshape(flat),
        jnp.swapaxes(kernel_two, 2, 3).reshape(flat),
    )
    mid = side - 2

    def cost(cells):
        flops = int(cells * wide * TAPS * TAPS * channels * channels * 8)
        return pl.CostEstimate(flops=flops, bytes_accessed=flops // 500, transcendentals=0)

    kept = [
        bf16((side * side * wide, channels)),
        bf16((mid * mid * wide, channels)),
        bf16((out_side * side * wide, channels)),
        bf16((mid * (mid + 4) * wide, channels)),
    ]

    def expert(messages, held, last):
        sums = [bf16((2 * TAPS * TAPS, channels, channels))]
        scratch = [
            pltpu.VMEM((mid * mid * wide, channels), jnp.float32),
            pltpu.VMEM((side * side * wide, channels), jnp.bfloat16),
        ]
        if last:
            scratch = [pltpu.VMEM(k.shape, k.dtype) for k in kept] + scratch
        result = pl.pallas_call(
            functools.partial(expert_kernel, part, slots, side, len(held) // 4, last),
            out_shape=[bf16((message, channels))] * part + (sums if last else kept),
            scratch_shapes=scratch,
            compiler_params=PARAMS,
            cost_estimate=cost(2.0 * (2 * mid * mid + out_side * out_side + side * side)),
            name="expert",
        )(*messages, *weights, *held)
        return result[:part], list(result[part:])

    backs, held = {}, []
    for chunk, messages in zip(chunks, arrived):
        last = chunk is chunks[-1]
        back, rest = expert(messages, held, last)
        returned = dict(zip(chunk, back))
        if not last:
            held = held + rest
            before = [mask for mask in chunk if mask]
            for mask in chunk:
                backs[mask] = exchange(mask, returned[mask])
    total, _ = lax.optimization_barrier((rest[0], [backs[mask] for mask in before]))
    for mask in nearer:
        backs[mask] = exchange(mask, returned[mask], [backs[m] for m in before])
    away = lax.ppermute(total, ("half", "replica"), SWAP_HOME)
    away, _ = lax.optimization_barrier((away, [backs[mask] for mask in chunks[1]]))
    away = jnp.where(core == 0, total, away)
    beside = lax.ppermute(away, "replica", [(0, 1), (1, 0)])
    grads = away.astype(jnp.float32) + beside.astype(jnp.float32)
    first_grad, second_grad = grads.reshape((2, 1, TAPS, TAPS, channels, channels))
    output, tiles_out, gate_grad = pl.pallas_call(
        functools.partial(unpack_kernel, slots, [*chunks[0], *nearer]),
        out_shape=[
            bf16(cotangent.shape),
            bf16(tiles_rows.shape),
            f32((1, patches)),
        ],
        compiler_params=PARAMS,
        name="unpack",
    )(key, gate_row, cotangent, *[backs[mask] for mask in [*chunks[0], *nearer]])
    tiles_grad = jnp.transpose(tiles_out.reshape(side, side, patches, channels), (2, 0, 1, 3))
    return (output, tiles_grad, first_grad, second_grad, gate_grad[0])


def solution(mesh):
    groups, experts, cores = (mesh.shape[a] for a in ("groups", "expert", "replica"))
    mesh = Mesh(
        mesh.devices.reshape(groups, cores, experts // cores, cores),
        ("groups", "half", "owner", "replica"),
    )
    every = ("groups", "half", "owner", "replica")
    placed = (
        P(every, None, None, None),
        P(every),
        P(every),
        P(("half", "owner"), None, None, None, None),
        P(("half", "owner"), None, None, None, None),
        P(every, None, None, None),
    )
    return jax.shard_map(
        shards,
        mesh=mesh,
        in_specs=placed,
        out_specs=(
            P(every, None, None, None),
            P(every, None, None, None),
            P(("groups", "half", "owner"), None, None, None, None),
            P(("groups", "half", "owner"), None, None, None, None),
            P(every),
        ),
        check_vma=False,
    )
```

```python
import functools

import jax
import jax.numpy as jnp
from jax import lax
from jax.experimental import pallas as pl
from jax.experimental.pallas import tpu as pltpu
from jax.sharding import Mesh
from jax.sharding import PartitionSpec as P

SWAP = [(0, 3), (2, 1)]
SWAP_HOME = [(1, 3), (3, 1)]
TAPS = 3
BLOCK = 8
PLACED = pl.BlockSpec(memory_space=pl.ANY)
PACK_PARAMS = pltpu.CompilerParams(vmem_limit_bytes=56 * 1024 * 1024)
PARAMS = pltpu.CompilerParams(vmem_limit_bytes=40 * 1024 * 1024)


def dot(left, right):
    return jnp.dot(left, right, preferred_element_type=jnp.float32)


def iota(shape, dim):
    return lax.broadcasted_iota(jnp.int32, shape, dim)


def onto_rows(row):
    count = row.shape[1]
    eye = iota((count, count), 0) == iota((count, count), 1)
    return jnp.sum(jnp.where(eye, row, 0.0), axis=1, keepdims=True)


def slot_matrix(key, slots, peers, cells_first):
    patches = key.shape[1]
    earlier = iota((patches, patches), 0) < iota((patches, patches), 1)
    same = onto_rows(key) == key
    rank = jnp.sum(jnp.where(same & earlier, 1.0, 0.0), axis=0, keepdims=True)
    code = key * 8.0 + rank
    columns = BLOCK * patches
    spread_row = iota((patches, columns), 0)
    spread_col = iota((patches, columns), 1)
    hit = (spread_col % patches) == spread_row if cells_first else (spread_col // BLOCK) == spread_row
    spread = jnp.where(hit, 1.0, 0.0)
    code_wide = jnp.sum(onto_rows(code) * spread, axis=0, keepdims=True)
    rows = peers * BLOCK * slots
    row = iota((rows, columns), 0)
    col = iota((rows, columns), 1)
    row_code = (row // (BLOCK * slots)) * 8 + row % slots
    row_cell = (row // slots) % BLOCK
    col_cell = col // patches if cells_first else col % BLOCK
    match = (row_code.astype(jnp.float32) == code_wide) & (row_cell == col_cell)
    return jnp.where(match, 1.0, 0.0).astype(jnp.bfloat16)


def pack_kernel(slots, place, route_at, gate_at, tiles_at, cot_at, *refs):
    route_ref, gate_ref, tiles_ref, cot_ref, sems = refs[-5:]
    *out_refs, pick_ref, cot_pick_ref = refs[:-5]
    peers = len(out_refs)
    step = BLOCK * slots
    pairs = ((route_at, route_ref), (gate_at, gate_ref), (tiles_at, tiles_ref), (cot_at, cot_ref))
    made = [pltpu.make_async_copy(a, b, sems.at[k]) for k, (a, b) in enumerate(pairs)]
    for copy in made:
        copy.start()
    made[0].wait()
    key = place(route_ref[...]).astype(jnp.float32)
    pick = slot_matrix(key, slots, peers, True)
    cot_pick = slot_matrix(key, slots, peers, False)
    pick_ref[...] = pick.T
    cot_pick_ref[...] = cot_pick.T
    made[1].wait()
    gate = onto_rows(gate_ref[...])[:, :, None]
    blocks = tiles_ref.shape[0]

    def put(at, values):
        values = values.astype(jnp.bfloat16)
        for peer in range(peers):
            out_refs[peer][at : at + step, :] = values[peer * step : (peer + 1) * step, :]

    made[2].wait()
    for block in range(blocks):
        put(block * step, dot(pick, tiles_ref[block]))
    made[3].wait()
    patches, rows, cols, channels = cot_ref.shape
    for i in range(rows):
        scaled = cot_ref[:, i, :, :].astype(jnp.float32) * gate
        scaled = scaled.reshape(patches * cols, channels).astype(jnp.bfloat16)
        put((blocks + i) * step, dot(cot_pick, scaled))


def unpack_kernel(slots, queue, pick_ref, cot_pick_ref, gate_ref, cot_ref, *refs):
    msgs, (out_ref, tiles_ref, gate_grad_ref) = refs[:-3], refs[-3:]
    msgs = [msgs[queue.index(peer)] for peer in range(len(msgs))]
    step = BLOCK * slots

    def gather(block):
        return jnp.concatenate([m[block * step : (block + 1) * step, :] for m in msgs], axis=0)

    blocks = tiles_ref.shape[0]
    for block in range(blocks):
        tiles_ref[block] = dot(pick_ref[...], gather(block)).astype(jnp.bfloat16)
    gate = onto_rows(gate_ref[...])[:, :, None]
    patches, rows, cols, channels = cot_ref.shape
    total = jnp.zeros((patches, cols, channels), jnp.float32)
    for i in range(rows):
        result = dot(cot_pick_ref[...], gather(blocks + i)).reshape(patches, cols, channels)
        out_ref[:, i, :, :] = (result * gate).astype(jnp.bfloat16)
        total = total + result * cot_ref[:, i, :, :].astype(jnp.float32)
    sums = jnp.sum(jnp.sum(total, axis=1), axis=1, keepdims=True)
    eye = iota((patches, patches), 0) == iota((patches, patches), 1)
    gate_grad_ref[...] = jnp.sum(jnp.where(eye, sums, 0.0), axis=0, keepdims=True)


def mix_matrix(peers, slots, inverse):
    size = peers * BLOCK * slots
    mixed, apart = (1, 0) if inverse else (0, 1)
    a = iota((size, size), mixed)
    b = iota((size, size), apart)
    cell_a, rest = a // (peers * slots), a % (peers * slots)
    from_b = (rest // slots) * (BLOCK * slots) + cell_a * slots + rest % slots
    return jnp.where(from_b == b, 1.0, 0.0).astype(jnp.bfloat16)


def expert_kernel(peers, slots, side, earlier, last, *refs):
    msgs = refs[:peers]
    one_ref, two_ref, one_t_ref, two_t_ref = refs[peers : peers + 4]
    held = [refs[peers + 4 + 4 * k : peers + 8 + 4 * k] for k in range(earlier)]
    outs = refs[peers + 4 + 4 * earlier :]
    backs = outs[:peers]
    sums_ref = outs[peers] if last else None
    x_ref, h_ref, g_ref, m_ref, slope_ref, t_ref = outs[-6:]
    step = BLOCK * slots
    wide = peers * slots
    mid, out = side - 2, side - 4
    blocks = side * side // BLOCK
    size = BLOCK * wide

    def gather(block):
        return jnp.concatenate([m[block * step : (block + 1) * step, :] for m in msgs], axis=0)

    def window(ref, cols, row, col, count):
        at = (row * cols + col) * wide
        return ref[at : at + count * wide, :]

    mix = mix_matrix(peers, slots, False)
    for block in range(blocks):
        x_ref[block * size : (block + 1) * size, :] = dot(mix, gather(block)).astype(jnp.bfloat16)
    for i in range(mid):
        lhs = jnp.concatenate(
            [window(x_ref, side, i + a, b, mid) for a in range(TAPS) for b in range(TAPS)], axis=1
        )
        pre = dot(lhs, one_ref[...])
        sigma = jax.nn.sigmoid(pre)
        rows = slice(i * mid * wide, (i + 1) * mid * wide)
        h_ref[rows, :] = (pre * sigma).astype(jnp.bfloat16)
        slope_ref[rows, :] = sigma * (1.0 + pre * (1.0 - sigma))

    apart = mix_matrix(peers, slots, True)

    def put(block, values):
        values = dot(apart, values).astype(jnp.bfloat16)
        for peer in range(peers):
            backs[peer][block * step : (block + 1) * step, :] = values[peer * step : (peer + 1) * step, :]

    for i in range(out):
        lhs = jnp.concatenate(
            [window(h_ref, mid, i + a, b, out) for a in range(TAPS) for b in range(TAPS)], axis=1
        )
        put(blocks + i, dot(lhs, two_ref[...]).astype(jnp.bfloat16))

    blank = jnp.zeros((2 * wide, x_ref.shape[1]), jnp.bfloat16)
    for i in range(out):
        at = i * (out + 4) * wide
        g_ref[at : at + 2 * wide, :] = blank
        g_ref[at + 2 * wide : at + 2 * wide + size, :] = dot(mix, gather(blocks + i)).astype(jnp.bfloat16)
        g_ref[at + 2 * wide + size : at + 4 * wide + size, :] = blank

    def transposed(ref, kernel_ref, rows, i):
        taps = [a for a in range(TAPS) if 0 <= i - a < rows]
        lhs = jnp.concatenate(
            [window(ref, rows + 4, i - a, 2 - b, rows + 2) for a in taps for b in range(TAPS)], axis=1
        )
        per = TAPS * x_ref.shape[1]
        return dot(lhs, kernel_ref[taps[0] * per : (taps[-1] + 1) * per, :])

    for i in range(mid):
        at = i * (mid + 4) * wide
        grad_mid = transposed(g_ref, two_t_ref, out, i) * slope_ref[i * mid * wide : (i + 1) * mid * wide, :]
        m_ref[at : at + 2 * wide, :] = blank
        m_ref[at + 2 * wide : at + (mid + 2) * wide, :] = grad_mid.astype(jnp.bfloat16)
        m_ref[at + (mid + 2) * wide : at + (mid + 4) * wide, :] = blank
    for i in range(side):
        t_ref[i * side * wide : (i + 1) * side * wide, :] = transposed(m_ref, one_t_ref, mid, i).astype(
            jnp.bfloat16
        )
    for block in range(blocks):
        put(block, t_ref[block * size : (block + 1) * size, :])


    if last:
        held = held + [(x_ref, h_ref, g_ref, m_ref)]
        kernel_sums([k[0] for k in held], side, [k[3] for k in held], mid, wide, sums_ref, 0)
        kernel_sums([k[1] for k in held], mid, [k[2] for k in held], out, wide, sums_ref, 1)


def kernel_sums(in_refs, cols, grad_refs, rows, wide, sums_ref, k):
    taps = TAPS * TAPS

    def window(ref, tap):
        a, b = divmod(tap, TAPS)
        starts = [((i + a) * cols + b) * wide for i in range(rows)]
        return [ref[at : at + rows * wide, :] for at in starts]

    grads = []
    for ref in grad_refs:
        starts = [(i * (rows + 4) + 2) * wide for i in range(rows)]
        grads = grads + [ref[at : at + rows * wide, :] for at in starts]
    grad_t = jnp.concatenate(grads, axis=0).T
    for first in range(0, taps, 2):
        pair = range(first, min(first + 2, taps))
        windows = [jnp.concatenate([w for ref in in_refs for w in window(ref, tap)], axis=0) for tap in pair]
        total = dot(grad_t, jnp.concatenate(windows, axis=1))
        channels = windows[0].shape[1]
        for j, tap in enumerate(pair):
            part = total[:, j * channels : (j + 1) * channels]
            sums_ref[k * taps + tap] = part.T.astype(jnp.bfloat16)


def shards(tiles, route, gate, conv_first, conv_second, cotangent):
    halves = lax.axis_size("half")
    per_half = lax.axis_size("owner")
    cores = lax.axis_size("replica")
    core = lax.axis_index("replica")
    peers = per_half * cores
    patches, side, _, channels = tiles.shape
    out_side = cotangent.shape[1]
    slots = max(2, (patches + peers - 1) // peers)
    blocks = side * side // BLOCK
    message = (side * side + out_side * out_side) * slots
    order = sorted(range(peers), key=lambda mask: (mask >= cores, -(mask // cores).bit_count(), mask % cores, mask))
    chunks = (order[: peers // 2], order[peers // 2 :])
    part = peers // 2
    wide = part * slots

    other_one, other_two = (
        lax.ppermute(k[0], ("half", "replica"), SWAP) for k in (conv_first, conv_second)
    )
    def place(route):
        home, owner = route // per_half, route % per_half
        here = lax.axis_index("owner") * cores + lax.axis_index("replica")
        return (owner * cores + (home + halves - lax.axis_index("half")) % halves) ^ here

    gate_row = gate[None, :]
    tiles_rows = jnp.transpose(tiles, (1, 2, 0, 3)).reshape(blocks, BLOCK * patches, channels)

    bf16 = functools.partial(jax.ShapeDtypeStruct, dtype=jnp.bfloat16)
    f32 = functools.partial(jax.ShapeDtypeStruct, dtype=jnp.float32)

    def exchange(mask, message, after=None):
        if mask == 0:
            return message
        if after is not None:
            message, _ = lax.optimization_barrier((message, after))
        return lax.ppermute(message, ("owner", "replica"), [(i, i ^ mask) for i in range(peers)])

    picks = [bf16((BLOCK * patches, peers * BLOCK * slots))] * 2
    *packed, pick, cot_pick = pl.pallas_call(
        functools.partial(pack_kernel, slots, place),
        in_specs=[PLACED] * 4,
        out_shape=[bf16((message, channels))] * peers + picks,
        scratch_shapes=[
            pltpu.VMEM((1, patches), jnp.int32),
            pltpu.VMEM((1, patches), jnp.float32),
            pltpu.VMEM(tiles_rows.shape, jnp.bfloat16),
            pltpu.VMEM(cotangent.shape, jnp.bfloat16),
            pltpu.SemaphoreType.DMA((4,)),
        ],
        compiler_params=PACK_PARAMS,
        name="pack",
    )(route[None, :], gate_row, tiles_rows, cotangent)

    nearer = sorted(chunks[1], key=lambda mask: (mask % cores, -mask))
    queue = [mask for mask in chunks[0] if mask >= cores] + order[1:cores] + nearer
    got = {0: packed[0]}
    for i, mask in enumerate(queue):
        got[mask] = exchange(mask, packed[mask], got[queue[0]] if i >= 4 else None)
    arrived = [[got[mask] for mask in chunk] for chunk in chunks]

    kernel_one = jnp.where(core == 0, conv_first[0], other_one)
    kernel_two = jnp.where(core == 0, conv_second[0], other_two)
    flat = (TAPS * TAPS * channels, channels)
    weights = (
        kernel_one.reshape(flat),
        kernel_two.reshape(flat),
        jnp.swapaxes(kernel_one, 2, 3).reshape(flat),
        jnp.swapaxes(kernel_two, 2, 3).reshape(flat),
    )
    mid = side - 2

    def cost(cells):
        flops = int(cells * wide * TAPS * TAPS * channels * channels * 8)
        return pl.CostEstimate(flops=flops, bytes_accessed=flops // 500, transcendentals=0)

    kept = [
        bf16((side * side * wide, channels)),
        bf16((mid * mid * wide, channels)),
        bf16((out_side * side * wide, channels)),
        bf16((mid * (mid + 4) * wide, channels)),
    ]

    def expert(messages, held, last):
        sums = [bf16((2 * TAPS * TAPS, channels, channels))]
        scratch = [
            pltpu.VMEM((mid * mid * wide, channels), jnp.float32),
            pltpu.VMEM((side * side * wide, channels), jnp.bfloat16),
        ]
        if last:
            scratch = [pltpu.VMEM(k.shape, k.dtype) for k in kept] + scratch
        result = pl.pallas_call(
            functools.partial(expert_kernel, part, slots, side, len(held) // 4, last),
            out_shape=[bf16((message, channels))] * part + (sums if last else kept),
            scratch_shapes=scratch,
            compiler_params=PARAMS,
            cost_estimate=cost(2.0 * (2 * mid * mid + out_side * out_side + side * side)),
            name="expert",
        )(*messages, *weights, *held)
        return result[:part], list(result[part:])

    backs, held = {}, []
    for chunk, messages in zip(chunks, arrived):
        last = chunk is chunks[-1]
        back, rest = expert(messages, held, last)
        returned = dict(zip(chunk, back))
        if not last:
            held = held + rest
            before = [mask for mask in chunk if mask]
            for mask in chunk:
                backs[mask] = exchange(mask, returned[mask])
    total, _ = lax.optimization_barrier((rest[0], [backs[mask] for mask in before]))
    for mask in nearer:
        backs[mask] = exchange(mask, returned[mask], [backs[m] for m in before])
    away = lax.ppermute(total, ("half", "replica"), SWAP_HOME)
    away, _ = lax.optimization_barrier((away, [backs[mask] for mask in chunks[1]]))
    away = jnp.where(core == 0, total, away)
    beside = lax.ppermute(away, "replica", [(0, 1), (1, 0)])
    grads = away.astype(jnp.float32) + beside.astype(jnp.float32)
    first_grad, second_grad = grads.reshape((2, 1, TAPS, TAPS, channels, channels))
    output, tiles_out, gate_grad = pl.pallas_call(
        functools.partial(unpack_kernel, slots, [*chunks[0], *nearer]),
        out_shape=[
            bf16(cotangent.shape),
            bf16(tiles_rows.shape),
            f32((1, patches)),
        ],
        compiler_params=PARAMS,
        name="unpack",
    )(pick, cot_pick, gate_row, cotangent, *[backs[mask] for mask in [*chunks[0], *nearer]])
    tiles_grad = jnp.transpose(tiles_out.reshape(side, side, patches, channels), (2, 0, 1, 3))
    return (output, tiles_grad, first_grad, second_grad, gate_grad[0])


def solution(mesh):
    groups, experts, cores = (mesh.shape[a] for a in ("groups", "expert", "replica"))
    mesh = Mesh(
        mesh.devices.reshape(groups, cores, experts // cores, cores),
        ("groups", "half", "owner", "replica"),
    )
    every = ("groups", "half", "owner", "replica")
    placed = (
        P(every, None, None, None),
        P(every),
        P(every),
        P(("half", "owner"), None, None, None, None),
        P(("half", "owner"), None, None, None, None),
        P(every, None, None, None),
    )
    return jax.shard_map(
        shards,
        mesh=mesh,
        in_specs=placed,
        out_specs=(
            P(every, None, None, None),
            P(every, None, None, None),
            P(("groups", "half", "owner"), None, None, None, None),
            P(("groups", "half", "owner"), None, None, None, None),
            P(every),
        ),
        check_vma=False,
    )
```

```python
import functools

import jax
import jax.numpy as jnp
from jax import lax
from jax.experimental import pallas as pl
from jax.experimental.pallas import tpu as pltpu
from jax.sharding import Mesh
from jax.sharding import PartitionSpec as P

SWAP = [(0, 3), (2, 1)]
SWAP_HOME = [(1, 3), (3, 1)]
TAPS = 3
ROWS = 5
BLOCK = 8
PLACED = pl.BlockSpec(memory_space=pl.ANY)
PACK_PARAMS = pltpu.CompilerParams(vmem_limit_bytes=56 * 1024 * 1024)
PARAMS = pltpu.CompilerParams(vmem_limit_bytes=40 * 1024 * 1024)


def dot(left, right):
    return jnp.dot(left, right, preferred_element_type=jnp.float32)


def iota(shape, dim):
    return lax.broadcasted_iota(jnp.int32, shape, dim)


def onto_rows(row):
    count = row.shape[1]
    eye = iota((count, count), 0) == iota((count, count), 1)
    return jnp.sum(jnp.where(eye, row, 0.0), axis=1, keepdims=True)


def slot_matrix(key, slots, peers, cells_first):
    patches = key.shape[1]
    earlier = iota((patches, patches), 0) < iota((patches, patches), 1)
    same = onto_rows(key) == key
    rank = jnp.sum(jnp.where(same & earlier, 1.0, 0.0), axis=0, keepdims=True)
    code = key * 8.0 + rank
    columns = BLOCK * patches
    spread_row = iota((patches, columns), 0)
    spread_col = iota((patches, columns), 1)
    hit = (spread_col % patches) == spread_row if cells_first else (spread_col // BLOCK) == spread_row
    spread = jnp.where(hit, 1.0, 0.0)
    code_wide = jnp.sum(onto_rows(code) * spread, axis=0, keepdims=True)
    rows = peers * BLOCK * slots
    row = iota((rows, columns), 0)
    col = iota((rows, columns), 1)
    row_code = (row // (BLOCK * slots)) * 8 + row % slots
    row_cell = (row // slots) % BLOCK
    col_cell = col // patches if cells_first else col % BLOCK
    match = (row_code.astype(jnp.float32) == code_wide) & (row_cell == col_cell)
    return jnp.where(match, 1.0, 0.0).astype(jnp.bfloat16)


def pack_kernel(slots, place, route_at, gate_at, tiles_at, cot_at, *refs):
    route_ref, gate_ref, tiles_ref, cot_ref, msg_ref, sems, out_sems = refs[-7:]
    *outs_at, pick_ref, cot_pick_ref = refs[:-7]
    peers = len(outs_at)
    step = BLOCK * slots
    pairs = ((route_at, route_ref), (gate_at, gate_ref), (tiles_at, tiles_ref), (cot_at, cot_ref))
    made = [pltpu.make_async_copy(a, b, sems.at[k]) for k, (a, b) in enumerate(pairs)]
    for copy in made:
        copy.start()
    made[0].wait()
    key = place(route_ref[...]).astype(jnp.float32)
    pick = slot_matrix(key, slots, peers, True)
    cot_pick = slot_matrix(key, slots, peers, False)
    pick_ref[...] = pick.T
    cot_pick_ref[...] = cot_pick.T
    made[1].wait()
    gate = onto_rows(gate_ref[...])[:, :, None]
    blocks = tiles_ref.shape[0]

    def put(at, values):
        values = values.astype(jnp.bfloat16)
        for peer in range(peers):
            msg_ref[peer, at : at + step, :] = values[peer * step : (peer + 1) * step, :]

    def leave(part, start, count):
        rows = pl.ds(start * step, count * step)
        sent = [
            pltpu.make_async_copy(msg_ref.at[peer, rows], outs_at[peer].at[rows], out_sems.at[part, peer])
            for peer in range(peers)
        ]
        for copy in sent:
            copy.start()
        return sent

    made[2].wait()
    for block in range(blocks):
        put(block * step, dot(pick, tiles_ref[block]))
    sent = leave(0, 0, blocks)
    made[3].wait()
    patches, rows, cols, channels = cot_ref.shape
    for i in range(rows):
        scaled = cot_ref[:, i, :, :].astype(jnp.float32) * gate
        scaled = scaled.reshape(patches * cols, channels).astype(jnp.bfloat16)
        put((blocks + i) * step, dot(cot_pick, scaled))
    for copy in sent + leave(1, blocks, rows):
        copy.wait()


def unpack_kernel(slots, queue, pick_ref, cot_pick_ref, gate_ref, cot_ref, *refs):
    msgs, (out_ref, tiles_ref, gate_grad_ref) = refs[:-3], refs[-3:]
    msgs = [msgs[queue.index(peer)] for peer in range(len(msgs))]
    step = BLOCK * slots

    def gather(block):
        return jnp.concatenate([m[block * step : (block + 1) * step, :] for m in msgs], axis=0)

    blocks = tiles_ref.shape[0]
    for block in range(blocks):
        tiles_ref[block] = dot(pick_ref[...], gather(block)).astype(jnp.bfloat16)
    gate = onto_rows(gate_ref[...])[:, :, None]
    patches, rows, cols, channels = cot_ref.shape
    total = jnp.zeros((patches, cols, channels), jnp.float32)
    for i in range(rows):
        result = dot(cot_pick_ref[...], gather(blocks + i)).reshape(patches, cols, channels)
        out_ref[:, i, :, :] = (result * gate).astype(jnp.bfloat16)
        total = total + result * cot_ref[:, i, :, :].astype(jnp.float32)
    sums = jnp.sum(jnp.sum(total, axis=1), axis=1, keepdims=True)
    eye = iota((patches, patches), 0) == iota((patches, patches), 1)
    gate_grad_ref[...] = jnp.sum(jnp.where(eye, sums, 0.0), axis=0, keepdims=True)


def mix_matrix(peers, slots, inverse):
    size = peers * BLOCK * slots
    mixed, apart = (1, 0) if inverse else (0, 1)
    a = iota((size, size), mixed)
    b = iota((size, size), apart)
    cell_a, rest = a // (peers * slots), a % (peers * slots)
    from_b = (rest // slots) * (BLOCK * slots) + cell_a * slots + rest % slots
    return jnp.where(from_b == b, 1.0, 0.0).astype(jnp.bfloat16)


def expert_kernel(peers, slots, side, earlier, last, *refs):
    msgs = refs[:peers]
    one_ref, two_ref, one_t_ref, two_t_ref = refs[peers : peers + 4]
    held = [refs[peers + 4 + 4 * k : peers + 8 + 4 * k] for k in range(earlier)]
    outs = refs[peers + 4 + 4 * earlier :]
    backs = outs[:peers]
    sums_ref = outs[peers] if last else None
    x_ref, h_ref, g_ref, m_ref, slope_ref, t_ref = outs[-6:]
    step = BLOCK * slots
    wide = peers * slots
    mid, out = side - 2, side - 4
    blocks = side * side // BLOCK
    size = BLOCK * wide

    def gather(block):
        return jnp.concatenate([m[block * step : (block + 1) * step, :] for m in msgs], axis=0)

    def groups(first, end):
        return [range(i, min(i + ROWS, end)) for i in range(first, end, ROWS)]

    def window(ref, cols, row, col, count):
        at = (row * cols + col) * wide
        return ref[at : at + count * wide, :]

    mix = mix_matrix(peers, slots, False)
    for block in range(blocks):
        x_ref[block * size : (block + 1) * size, :] = dot(mix, gather(block)).astype(jnp.bfloat16)
    def lined(ref, cols, rows, count):
        taps = [(a, b) for a in range(TAPS) for b in range(TAPS)]
        lines = [
            jnp.concatenate([window(ref, cols, i + a, b, count) for a, b in taps], axis=1) for i in rows
        ]
        return jnp.concatenate(lines, axis=0)

    for group in groups(0, mid):
        pre = dot(lined(x_ref, side, group, mid), one_ref[...])
        sigma = jax.nn.sigmoid(pre)
        rows = slice(group[0] * mid * wide, (group[-1] + 1) * mid * wide)
        h_ref[rows, :] = (pre * sigma).astype(jnp.bfloat16)
        slope_ref[rows, :] = sigma * (1.0 + pre * (1.0 - sigma))

    apart = mix_matrix(peers, slots, True)

    def put(block, values):
        values = dot(apart, values).astype(jnp.bfloat16)
        for peer in range(peers):
            backs[peer][block * step : (block + 1) * step, :] = values[peer * step : (peer + 1) * step, :]

    for group in groups(0, out):
        result = dot(lined(h_ref, mid, group, out), two_ref[...]).astype(jnp.bfloat16)
        for k, i in enumerate(group):
            put(blocks + i, result[k * size : (k + 1) * size, :])

    blank = jnp.zeros((2 * wide, x_ref.shape[1]), jnp.bfloat16)
    for i in range(out):
        at = i * (out + 4) * wide
        g_ref[at : at + 2 * wide, :] = blank
        g_ref[at + 2 * wide : at + 2 * wide + size, :] = dot(mix, gather(blocks + i)).astype(jnp.bfloat16)
        g_ref[at + 2 * wide + size : at + 4 * wide + size, :] = blank

    def transposed(ref, kernel_ref, rows, group):
        taps = [a for a in range(TAPS) if 0 <= group[0] - a < rows]
        lines = [
            jnp.concatenate(
                [window(ref, rows + 4, i - a, 2 - b, rows + 2) for a in taps for b in range(TAPS)], axis=1
            )
            for i in group
        ]
        per = TAPS * x_ref.shape[1]
        lhs = jnp.concatenate(lines, axis=0)
        return dot(lhs, kernel_ref[taps[0] * per : (taps[-1] + 1) * per, :])

    def edged(rows):
        return [range(i, i + 1) for i in (0, 1)] + groups(2, rows) + [range(i, i + 1) for i in (rows, rows + 1)]

    for group in edged(out):
        rows = slice(group[0] * mid * wide, (group[-1] + 1) * mid * wide)
        grad_mid = (transposed(g_ref, two_t_ref, out, group) * slope_ref[rows, :]).astype(jnp.bfloat16)
        for k, i in enumerate(group):
            at = i * (mid + 4) * wide
            m_ref[at : at + 2 * wide, :] = blank
            m_ref[at + 2 * wide : at + (mid + 2) * wide, :] = grad_mid[k * mid * wide : (k + 1) * mid * wide, :]
            m_ref[at + (mid + 2) * wide : at + (mid + 4) * wide, :] = blank
    for group in edged(mid):
        rows = slice(group[0] * side * wide, (group[-1] + 1) * side * wide)
        t_ref[rows, :] = transposed(m_ref, one_t_ref, mid, group).astype(jnp.bfloat16)
    for block in range(blocks):
        put(block, t_ref[block * size : (block + 1) * size, :])


    if last:
        held = held + [(x_ref, h_ref, g_ref, m_ref)]
        kernel_sums([k[0] for k in held], side, [k[3] for k in held], mid, wide, sums_ref, 0)
        kernel_sums([k[1] for k in held], mid, [k[2] for k in held], out, wide, sums_ref, 1)


def kernel_sums(in_refs, cols, grad_refs, rows, wide, sums_ref, k):
    taps = TAPS * TAPS

    def window(ref, tap):
        a, b = divmod(tap, TAPS)
        starts = [((i + a) * cols + b) * wide for i in range(rows)]
        return [ref[at : at + rows * wide, :] for at in starts]

    grads = []
    for ref in grad_refs:
        starts = [(i * (rows + 4) + 2) * wide for i in range(rows)]
        grads = grads + [ref[at : at + rows * wide, :] for at in starts]
    grad_t = jnp.concatenate(grads, axis=0).T
    for first in range(0, taps, 2):
        pair = range(first, min(first + 2, taps))
        windows = [jnp.concatenate([w for ref in in_refs for w in window(ref, tap)], axis=0) for tap in pair]
        total = dot(grad_t, jnp.concatenate(windows, axis=1))
        channels = windows[0].shape[1]
        for j, tap in enumerate(pair):
            part = total[:, j * channels : (j + 1) * channels]
            sums_ref[k * taps + tap] = part.T.astype(jnp.bfloat16)


def shards(tiles, route, gate, conv_first, conv_second, cotangent):
    halves = lax.axis_size("half")
    per_half = lax.axis_size("owner")
    cores = lax.axis_size("replica")
    core = lax.axis_index("replica")
    peers = per_half * cores
    patches, side, _, channels = tiles.shape
    out_side = cotangent.shape[1]
    slots = max(2, (patches + peers - 1) // peers)
    blocks = side * side // BLOCK
    message = (side * side + out_side * out_side) * slots
    order = sorted(range(peers), key=lambda mask: (mask >= cores, -(mask // cores).bit_count(), mask % cores, mask))
    chunks = (order[: peers // 2], order[peers // 2 :])
    part = peers // 2
    wide = part * slots

    other_one, other_two = (
        lax.ppermute(k[0], ("half", "replica"), SWAP) for k in (conv_first, conv_second)
    )
    def place(route):
        home, owner = route // per_half, route % per_half
        here = lax.axis_index("owner") * cores + lax.axis_index("replica")
        return (owner * cores + (home + halves - lax.axis_index("half")) % halves) ^ here

    gate_row = gate[None, :]
    tiles_rows = jnp.transpose(tiles, (1, 2, 0, 3)).reshape(blocks, BLOCK * patches, channels)

    bf16 = functools.partial(jax.ShapeDtypeStruct, dtype=jnp.bfloat16)
    f32 = functools.partial(jax.ShapeDtypeStruct, dtype=jnp.float32)

    def exchange(mask, message, after=None):
        if mask == 0:
            return message
        if after is not None:
            message, _ = lax.optimization_barrier((message, after))
        return lax.ppermute(message, ("owner", "replica"), [(i, i ^ mask) for i in range(peers)])

    picks = [bf16((BLOCK * patches, peers * BLOCK * slots))] * 2
    *packed, pick, cot_pick = pl.pallas_call(
        functools.partial(pack_kernel, slots, place),
        in_specs=[PLACED] * 4,
        out_specs=[PLACED] * peers + [pl.BlockSpec()] * 2,
        out_shape=[bf16((message, channels))] * peers + picks,
        scratch_shapes=[
            pltpu.VMEM((1, patches), jnp.int32),
            pltpu.VMEM((1, patches), jnp.float32),
            pltpu.VMEM(tiles_rows.shape, jnp.bfloat16),
            pltpu.VMEM(cotangent.shape, jnp.bfloat16),
            pltpu.VMEM((peers, message, channels), jnp.bfloat16),
            pltpu.SemaphoreType.DMA((4,)),
            pltpu.SemaphoreType.DMA((2, peers)),
        ],
        compiler_params=PACK_PARAMS,
        name="pack",
    )(route[None, :], gate_row, tiles_rows, cotangent)

    nearer = sorted(chunks[1], key=lambda mask: (mask % cores, -mask))
    queue = [mask for mask in chunks[0] if mask >= cores] + order[1:cores] + nearer
    got = {0: packed[0]}
    for i, mask in enumerate(queue):
        got[mask] = exchange(mask, packed[mask], got[queue[0]] if i >= 4 else None)
    arrived = [[got[mask] for mask in chunk] for chunk in chunks]

    kernel_one = jnp.where(core == 0, conv_first[0], other_one)
    kernel_two = jnp.where(core == 0, conv_second[0], other_two)
    flat = (TAPS * TAPS * channels, channels)
    weights = (
        kernel_one.reshape(flat),
        kernel_two.reshape(flat),
        jnp.swapaxes(kernel_one, 2, 3).reshape(flat),
        jnp.swapaxes(kernel_two, 2, 3).reshape(flat),
    )
    mid = side - 2

    def cost(cells):
        flops = int(cells * wide * TAPS * TAPS * channels * channels * 8)
        return pl.CostEstimate(flops=flops, bytes_accessed=flops // 500, transcendentals=0)

    kept = [
        bf16((side * side * wide, channels)),
        bf16((mid * mid * wide, channels)),
        bf16((out_side * side * wide, channels)),
        bf16((mid * (mid + 4) * wide, channels)),
    ]

    def expert(messages, held, last):
        sums = [bf16((2 * TAPS * TAPS, channels, channels))]
        scratch = [
            pltpu.VMEM((mid * mid * wide, channels), jnp.float32),
            pltpu.VMEM((side * side * wide, channels), jnp.bfloat16),
        ]
        if last:
            scratch = [pltpu.VMEM(k.shape, k.dtype) for k in kept] + scratch
        result = pl.pallas_call(
            functools.partial(expert_kernel, part, slots, side, len(held) // 4, last),
            out_shape=[bf16((message, channels))] * part + (sums if last else kept),
            scratch_shapes=scratch,
            compiler_params=PARAMS,
            cost_estimate=cost(2.0 * (2 * mid * mid + out_side * out_side + side * side)),
            name="expert",
        )(*messages, *weights, *held)
        return result[:part], list(result[part:])

    backs, held = {}, []
    for chunk, messages in zip(chunks, arrived):
        last = chunk is chunks[-1]
        back, rest = expert(messages, held, last)
        returned = dict(zip(chunk, back))
        if not last:
            held = held + rest
            before = [mask for mask in chunk if mask]
            for mask in chunk:
                backs[mask] = exchange(mask, returned[mask])
    total, _ = lax.optimization_barrier((rest[0], [backs[mask] for mask in before]))
    for mask in nearer:
        backs[mask] = exchange(mask, returned[mask], [backs[m] for m in before])
    away = lax.ppermute(total, ("half", "replica"), SWAP_HOME)
    away, _ = lax.optimization_barrier((away, [backs[mask] for mask in chunks[1]]))
    away = jnp.where(core == 0, total, away)
    beside = lax.ppermute(away, "replica", [(0, 1), (1, 0)])
    grads = away.astype(jnp.float32) + beside.astype(jnp.float32)
    first_grad, second_grad = grads.reshape((2, 1, TAPS, TAPS, channels, channels))
    output, tiles_out, gate_grad = pl.pallas_call(
        functools.partial(unpack_kernel, slots, [*chunks[0], *nearer]),
        out_shape=[
            bf16(cotangent.shape),
            bf16(tiles_rows.shape),
            f32((1, patches)),
        ],
        compiler_params=PARAMS,
        name="unpack",
    )(pick, cot_pick, gate_row, cotangent, *[backs[mask] for mask in [*chunks[0], *nearer]])
    tiles_grad = jnp.transpose(tiles_out.reshape(side, side, patches, channels), (2, 0, 1, 3))
    return (output, tiles_grad, first_grad, second_grad, gate_grad[0])


def solution(mesh):
    groups, experts, cores = (mesh.shape[a] for a in ("groups", "expert", "replica"))
    mesh = Mesh(
        mesh.devices.reshape(groups, cores, experts // cores, cores),
        ("groups", "half", "owner", "replica"),
    )
    every = ("groups", "half", "owner", "replica")
    placed = (
        P(every, None, None, None),
        P(every),
        P(every),
        P(("half", "owner"), None, None, None, None),
        P(("half", "owner"), None, None, None, None),
        P(every, None, None, None),
    )
    return jax.shard_map(
        shards,
        mesh=mesh,
        in_specs=placed,
        out_specs=(
            P(every, None, None, None),
            P(every, None, None, None),
            P(("groups", "half", "owner"), None, None, None, None),
            P(("groups", "half", "owner"), None, None, None, None),
            P(every),
        ),
        check_vma=False,
    )
```

```python
import functools

import jax
import jax.numpy as jnp
from jax import lax
from jax.experimental import pallas as pl
from jax.experimental.pallas import tpu as pltpu
from jax.sharding import Mesh
from jax.sharding import PartitionSpec as P

SWAP = [(0, 3), (2, 1)]
SWAP_HOME = [(1, 3), (3, 1)]
TAPS = 3
ROWS = 4
BLOCK = 8
PLACED = pl.BlockSpec(memory_space=pl.ANY)
PACK_PARAMS = pltpu.CompilerParams(vmem_limit_bytes=56 * 1024 * 1024)
PARAMS = pltpu.CompilerParams(vmem_limit_bytes=40 * 1024 * 1024)


def dot(left, right):
    return jnp.dot(left, right, preferred_element_type=jnp.float32)


def iota(shape, dim):
    return lax.broadcasted_iota(jnp.int32, shape, dim)


def onto_rows(row):
    count = row.shape[1]
    eye = iota((count, count), 0) == iota((count, count), 1)
    return jnp.sum(jnp.where(eye, row, 0.0), axis=1, keepdims=True)


def slot_matrix(key, slots, peers, cells_first):
    patches = key.shape[1]
    earlier = iota((patches, patches), 0) < iota((patches, patches), 1)
    same = onto_rows(key) == key
    rank = jnp.sum(jnp.where(same & earlier, 1.0, 0.0), axis=0, keepdims=True)
    code = key * 8.0 + rank
    columns = BLOCK * patches
    spread_row = iota((patches, columns), 0)
    spread_col = iota((patches, columns), 1)
    hit = (spread_col % patches) == spread_row if cells_first else (spread_col // BLOCK) == spread_row
    spread = jnp.where(hit, 1.0, 0.0)
    code_wide = jnp.sum(onto_rows(code) * spread, axis=0, keepdims=True)
    rows = peers * BLOCK * slots
    row = iota((rows, columns), 0)
    col = iota((rows, columns), 1)
    row_code = (row // (BLOCK * slots)) * 8 + row % slots
    row_cell = (row // slots) % BLOCK
    col_cell = col // patches if cells_first else col % BLOCK
    match = (row_code.astype(jnp.float32) == code_wide) & (row_cell == col_cell)
    return jnp.where(match, 1.0, 0.0).astype(jnp.bfloat16)


def pack_kernel(slots, place, route_at, gate_at, tiles_at, cot_at, *refs):
    route_ref, gate_ref, tiles_ref, cot_ref, msg_ref, sems, out_sems = refs[-7:]
    *outs_at, pick_ref, cot_pick_ref = refs[:-7]
    peers = len(outs_at)
    step = BLOCK * slots
    pairs = ((route_at, route_ref), (gate_at, gate_ref), (tiles_at, tiles_ref), (cot_at, cot_ref))
    made = [pltpu.make_async_copy(a, b, sems.at[k]) for k, (a, b) in enumerate(pairs)]
    for copy in made:
        copy.start()
    made[0].wait()
    key = place(route_ref[...]).astype(jnp.float32)
    pick = slot_matrix(key, slots, peers, True)
    cot_pick = slot_matrix(key, slots, peers, False)
    pick_ref[...] = pick.T
    cot_pick_ref[...] = cot_pick.T
    made[1].wait()
    gate = onto_rows(gate_ref[...])[:, :, None]
    blocks = tiles_ref.shape[0]

    def put(at, values):
        values = values.astype(jnp.bfloat16)
        for peer in range(peers):
            msg_ref[peer, at : at + step, :] = values[peer * step : (peer + 1) * step, :]

    def leave(part, start, count):
        rows = pl.ds(start * step, count * step)
        sent = [
            pltpu.make_async_copy(msg_ref.at[peer, rows], outs_at[peer].at[rows], out_sems.at[part, peer])
            for peer in range(peers)
        ]
        for copy in sent:
            copy.start()
        return sent

    made[2].wait()
    for block in range(blocks):
        put(block * step, dot(pick, tiles_ref[block]))
    sent = leave(0, 0, blocks)
    made[3].wait()
    patches, rows, cols, channels = cot_ref.shape
    for i in range(rows):
        scaled = cot_ref[:, i, :, :].astype(jnp.float32) * gate
        scaled = scaled.reshape(patches * cols, channels).astype(jnp.bfloat16)
        put((blocks + i) * step, dot(cot_pick, scaled))
    for copy in sent + leave(1, blocks, rows):
        copy.wait()


def unpack_kernel(slots, queue, pick_ref, cot_pick_ref, gate_ref, cot_ref, *refs):
    msgs, (out_ref, tiles_ref, gate_grad_ref) = refs[:-3], refs[-3:]
    msgs = [msgs[queue.index(peer)] for peer in range(len(msgs))]
    step = BLOCK * slots

    def gather(block):
        return jnp.concatenate([m[block * step : (block + 1) * step, :] for m in msgs], axis=0)

    blocks = tiles_ref.shape[0]
    for block in range(blocks):
        tiles_ref[block] = dot(pick_ref[...], gather(block)).astype(jnp.bfloat16)
    gate = onto_rows(gate_ref[...])[:, :, None]
    patches, rows, cols, channels = cot_ref.shape
    total = jnp.zeros((patches, cols, channels), jnp.float32)
    for i in range(rows):
        result = dot(cot_pick_ref[...], gather(blocks + i)).reshape(patches, cols, channels)
        out_ref[:, i, :, :] = (result * gate).astype(jnp.bfloat16)
        total = total + result * cot_ref[:, i, :, :].astype(jnp.float32)
    sums = jnp.sum(jnp.sum(total, axis=1), axis=1, keepdims=True)
    eye = iota((patches, patches), 0) == iota((patches, patches), 1)
    gate_grad_ref[...] = jnp.sum(jnp.where(eye, sums, 0.0), axis=0, keepdims=True)


def mix_matrix(peers, slots, inverse):
    size = peers * BLOCK * slots
    mixed, apart = (1, 0) if inverse else (0, 1)
    a = iota((size, size), mixed)
    b = iota((size, size), apart)
    cell_a, rest = a // (peers * slots), a % (peers * slots)
    from_b = (rest // slots) * (BLOCK * slots) + cell_a * slots + rest % slots
    return jnp.where(from_b == b, 1.0, 0.0).astype(jnp.bfloat16)


def expert_kernel(peers, slots, side, earlier, last, *refs):
    msgs = refs[:peers]
    one_ref, two_ref, one_t_ref, two_t_ref = refs[peers : peers + 4]
    held = [refs[peers + 4 + 4 * k : peers + 8 + 4 * k] for k in range(earlier)]
    outs = refs[peers + 4 + 4 * earlier :]
    backs = outs[:peers]
    sums_ref = outs[peers] if last else None
    x_ref, h_ref, g_ref, m_ref, slope_ref, t_ref = outs[-6:]
    step = BLOCK * slots
    wide = peers * slots
    mid, out = side - 2, side - 4
    blocks = side * side // BLOCK
    size = BLOCK * wide

    def gather(block):
        return jnp.concatenate([m[block * step : (block + 1) * step, :] for m in msgs], axis=0)

    def groups(first, end):
        return [range(i, min(i + ROWS, end)) for i in range(first, end, ROWS)]

    def window(ref, cols, row, col, count):
        at = (row * cols + col) * wide
        return ref[at : at + count * wide, :]

    mix = mix_matrix(peers, slots, False)
    for block in range(blocks):
        x_ref[block * size : (block + 1) * size, :] = dot(mix, gather(block)).astype(jnp.bfloat16)
    def lined(ref, cols, rows, count):
        taps = [(a, b) for a in range(TAPS) for b in range(TAPS)]
        lines = [
            jnp.concatenate([window(ref, cols, i + a, b, count) for a, b in taps], axis=1) for i in rows
        ]
        return jnp.concatenate(lines, axis=0)

    for group in groups(0, mid):
        pre = dot(lined(x_ref, side, group, mid), one_ref[...])
        sigma = jax.nn.sigmoid(pre)
        rows = slice(group[0] * mid * wide, (group[-1] + 1) * mid * wide)
        h_ref[rows, :] = (pre * sigma).astype(jnp.bfloat16)
        slope_ref[rows, :] = sigma * (1.0 + pre * (1.0 - sigma))

    apart = mix_matrix(peers, slots, True)

    def put(block, values):
        values = dot(apart, values).astype(jnp.bfloat16)
        for peer in range(peers):
            backs[peer][block * step : (block + 1) * step, :] = values[peer * step : (peer + 1) * step, :]

    for group in groups(0, out):
        result = dot(lined(h_ref, mid, group, out), two_ref[...]).astype(jnp.bfloat16)
        for k, i in enumerate(group):
            put(blocks + i, result[k * size : (k + 1) * size, :])

    blank = jnp.zeros((2 * wide, x_ref.shape[1]), jnp.bfloat16)
    for i in range(out):
        at = i * (out + 4) * wide
        g_ref[at : at + 2 * wide, :] = blank
        g_ref[at + 2 * wide : at + 2 * wide + size, :] = dot(mix, gather(blocks + i)).astype(jnp.bfloat16)
        g_ref[at + 2 * wide + size : at + 4 * wide + size, :] = blank

    def transposed(ref, kernel_ref, rows, group):
        taps = [a for a in range(TAPS) if 0 <= group[0] - a < rows]
        lines = [
            jnp.concatenate(
                [window(ref, rows + 4, i - a, 2 - b, rows + 2) for a in taps for b in range(TAPS)], axis=1
            )
            for i in group
        ]
        per = TAPS * x_ref.shape[1]
        lhs = jnp.concatenate(lines, axis=0)
        return dot(lhs, kernel_ref[taps[0] * per : (taps[-1] + 1) * per, :])

    def edged(rows):
        return [range(i, i + 1) for i in (0, 1)] + groups(2, rows) + [range(i, i + 1) for i in (rows, rows + 1)]

    for group in edged(out):
        rows = slice(group[0] * mid * wide, (group[-1] + 1) * mid * wide)
        grad_mid = (transposed(g_ref, two_t_ref, out, group) * slope_ref[rows, :]).astype(jnp.bfloat16)
        for k, i in enumerate(group):
            at = i * (mid + 4) * wide
            m_ref[at : at + 2 * wide, :] = blank
            m_ref[at + 2 * wide : at + (mid + 2) * wide, :] = grad_mid[k * mid * wide : (k + 1) * mid * wide, :]
            m_ref[at + (mid + 2) * wide : at + (mid + 4) * wide, :] = blank
    for group in edged(mid):
        rows = slice(group[0] * side * wide, (group[-1] + 1) * side * wide)
        t_ref[rows, :] = transposed(m_ref, one_t_ref, mid, group).astype(jnp.bfloat16)
    for block in range(blocks):
        put(block, t_ref[block * size : (block + 1) * size, :])


    if last:
        held = held + [(x_ref, h_ref, g_ref, m_ref)]
        kernel_sums([k[0] for k in held], side, [k[3] for k in held], mid, wide, sums_ref, 0)
        kernel_sums([k[1] for k in held], mid, [k[2] for k in held], out, wide, sums_ref, 1)


def kernel_sums(in_refs, cols, grad_refs, rows, wide, sums_ref, k):
    taps = TAPS * TAPS

    def window(ref, tap):
        a, b = divmod(tap, TAPS)
        starts = [((i + a) * cols + b) * wide for i in range(rows)]
        return [ref[at : at + rows * wide, :] for at in starts]

    grads = []
    for ref in grad_refs:
        starts = [(i * (rows + 4) + 2) * wide for i in range(rows)]
        grads = grads + [ref[at : at + rows * wide, :] for at in starts]
    grad_t = jnp.concatenate(grads, axis=0).T
    for first in range(0, taps, 2):
        pair = range(first, min(first + 2, taps))
        windows = [jnp.concatenate([w for ref in in_refs for w in window(ref, tap)], axis=0) for tap in pair]
        total = dot(grad_t, jnp.concatenate(windows, axis=1))
        channels = windows[0].shape[1]
        for j, tap in enumerate(pair):
            part = total[:, j * channels : (j + 1) * channels]
            sums_ref[k * taps + tap] = part.T.astype(jnp.bfloat16)


def shards(tiles, route, gate, conv_first, conv_second, cotangent):
    halves = lax.axis_size("half")
    per_half = lax.axis_size("owner")
    cores = lax.axis_size("replica")
    core = lax.axis_index("replica")
    peers = per_half * cores
    patches, side, _, channels = tiles.shape
    out_side = cotangent.shape[1]
    slots = max(2, (patches + peers - 1) // peers)
    blocks = side * side // BLOCK
    message = (side * side + out_side * out_side) * slots
    order = sorted(range(peers), key=lambda mask: (mask >= cores, -(mask // cores).bit_count(), mask % cores, mask))
    chunks = (order[: peers // 2], order[peers // 2 :])
    part = peers // 2
    wide = part * slots

    other_one, other_two = (
        lax.ppermute(k[0], ("half", "replica"), SWAP) for k in (conv_first, conv_second)
    )
    def place(route):
        home, owner = route // per_half, route % per_half
        here = lax.axis_index("owner") * cores + lax.axis_index("replica")
        return (owner * cores + (home + halves - lax.axis_index("half")) % halves) ^ here

    gate_row = gate[None, :]
    tiles_rows = jnp.transpose(tiles, (1, 2, 0, 3)).reshape(blocks, BLOCK * patches, channels)

    bf16 = functools.partial(jax.ShapeDtypeStruct, dtype=jnp.bfloat16)
    f32 = functools.partial(jax.ShapeDtypeStruct, dtype=jnp.float32)

    def exchange(mask, message, after=None):
        if mask == 0:
            return message
        if after is not None:
            message, _ = lax.optimization_barrier((message, after))
        return lax.ppermute(message, ("owner", "replica"), [(i, i ^ mask) for i in range(peers)])

    picks = [bf16((BLOCK * patches, peers * BLOCK * slots))] * 2
    *packed, pick, cot_pick = pl.pallas_call(
        functools.partial(pack_kernel, slots, place),
        in_specs=[PLACED] * 4,
        out_specs=[PLACED] * peers + [pl.BlockSpec()] * 2,
        out_shape=[bf16((message, channels))] * peers + picks,
        scratch_shapes=[
            pltpu.VMEM((1, patches), jnp.int32),
            pltpu.VMEM((1, patches), jnp.float32),
            pltpu.VMEM(tiles_rows.shape, jnp.bfloat16),
            pltpu.VMEM(cotangent.shape, jnp.bfloat16),
            pltpu.VMEM((peers, message, channels), jnp.bfloat16),
            pltpu.SemaphoreType.DMA((4,)),
            pltpu.SemaphoreType.DMA((2, peers)),
        ],
        compiler_params=PACK_PARAMS,
        name="pack",
    )(route[None, :], gate_row, tiles_rows, cotangent)

    nearer = sorted(chunks[1], key=lambda mask: (mask % cores, -mask))
    queue = [mask for mask in chunks[0] if mask >= cores] + order[1:cores] + nearer
    got = {0: packed[0]}
    for i, mask in enumerate(queue):
        got[mask] = exchange(mask, packed[mask], got[queue[0]] if i >= 4 else None)
    arrived = [[got[mask] for mask in chunk] for chunk in chunks]

    kernel_one = jnp.where(core == 0, conv_first[0], other_one)
    kernel_two = jnp.where(core == 0, conv_second[0], other_two)
    flat = (TAPS * TAPS * channels, channels)
    weights = (
        kernel_one.reshape(flat),
        kernel_two.reshape(flat),
        jnp.swapaxes(kernel_one, 2, 3).reshape(flat),
        jnp.swapaxes(kernel_two, 2, 3).reshape(flat),
    )
    mid = side - 2

    def cost(cells):
        flops = int(cells * wide * TAPS * TAPS * channels * channels * 8)
        return pl.CostEstimate(flops=flops, bytes_accessed=flops // 500, transcendentals=0)

    kept = [
        bf16((side * side * wide, channels)),
        bf16((mid * mid * wide, channels)),
        bf16((out_side * side * wide, channels)),
        bf16((mid * (mid + 4) * wide, channels)),
    ]

    def expert(messages, held, last):
        sums = [bf16((2 * TAPS * TAPS, channels, channels))]
        scratch = [
            pltpu.VMEM((mid * mid * wide, channels), jnp.float32),
            pltpu.VMEM((side * side * wide, channels), jnp.bfloat16),
        ]
        if last:
            scratch = [pltpu.VMEM(k.shape, k.dtype) for k in kept] + scratch
        result = pl.pallas_call(
            functools.partial(expert_kernel, part, slots, side, len(held) // 4, last),
            out_shape=[bf16((message, channels))] * part + (sums if last else kept),
            scratch_shapes=scratch,
            compiler_params=PARAMS,
            cost_estimate=cost(2.0 * (2 * mid * mid + out_side * out_side + side * side)),
            name="expert",
        )(*messages, *weights, *held)
        return result[:part], list(result[part:])

    backs, held = {}, []
    for chunk, messages in zip(chunks, arrived):
        last = chunk is chunks[-1]
        back, rest = expert(messages, held, last)
        returned = dict(zip(chunk, back))
        if not last:
            held = held + rest
            before = [mask for mask in chunk if mask]
            for mask in chunk:
                backs[mask] = exchange(mask, returned[mask])
    total, _ = lax.optimization_barrier((rest[0], [backs[mask] for mask in before]))
    for mask in nearer:
        backs[mask] = exchange(mask, returned[mask], [backs[m] for m in before])
    away = lax.ppermute(total, ("half", "replica"), SWAP_HOME)
    away, _ = lax.optimization_barrier((away, [backs[mask] for mask in chunks[1]]))
    away = jnp.where(core == 0, total, away)
    beside = lax.ppermute(away, "replica", [(0, 1), (1, 0)])
    grads = away.astype(jnp.float32) + beside.astype(jnp.float32)
    first_grad, second_grad = grads.reshape((2, 1, TAPS, TAPS, channels, channels))
    output, tiles_out, gate_grad = pl.pallas_call(
        functools.partial(unpack_kernel, slots, [*chunks[0], *nearer]),
        out_shape=[
            bf16(cotangent.shape),
            bf16(tiles_rows.shape),
            f32((1, patches)),
        ],
        compiler_params=PARAMS,
        name="unpack",
    )(pick, cot_pick, gate_row, cotangent, *[backs[mask] for mask in [*chunks[0], *nearer]])
    tiles_grad = jnp.transpose(tiles_out.reshape(side, side, patches, channels), (2, 0, 1, 3))
    return (output, tiles_grad, first_grad, second_grad, gate_grad[0])


def solution(mesh):
    groups, experts, cores = (mesh.shape[a] for a in ("groups", "expert", "replica"))
    mesh = Mesh(
        mesh.devices.reshape(groups, cores, experts // cores, cores),
        ("groups", "half", "owner", "replica"),
    )
    every = ("groups", "half", "owner", "replica")
    placed = (
        P(every, None, None, None),
        P(every),
        P(every),
        P(("half", "owner"), None, None, None, None),
        P(("half", "owner"), None, None, None, None),
        P(every, None, None, None),
    )
    return jax.shard_map(
        shards,
        mesh=mesh,
        in_specs=placed,
        out_specs=(
            P(every, None, None, None),
            P(every, None, None, None),
            P(("groups", "half", "owner"), None, None, None, None),
            P(("groups", "half", "owner"), None, None, None, None),
            P(every),
        ),
        check_vma=False,
    )
```
